256 devices in a mesh: gx: 32 (over z, y), gy: 8 (over x, core).
Axes of the slice: x: 4, y: 4, z: 8, core: 2. Of those that a mesh axis runs over, the one named last changes fastest.
Arguments:
- cells: int32 [3, 524288], P(None, ('gx', 'gy')), may hold values from 0 to 511, as said below
- offsets: float32 [3, 524288], P(None, ('gx', 'gy')), may hold values from 0 to 1
- charges: float32 [524288], P(('gx', 'gy')), may hold values from -4 to 4
- kernel_weights: float32 [4, 3], replicated, may hold values from 0.25 to 1
- screening: float32 [1], replicated, may hold values from 0.1 to 0.4
Outputs:
- potential: float32 [524288], P(('gx', 'gy'))
- forces: float32 [3, 524288], P(None, ('gx', 'gy'))
The draws below stay inside these ranges and needn't reach their ends.
Inputs may be any that keep to these rules, and one draw needn't show every extreme that they name: The particles of one device lie in that device's block of 16 x 32 x 512 fine cells and are sorted by cell; every device has a particle in the first and in the last cell of its block.
All inputs are finite; a program needn't handle non-finite values.
Results may differ from the reference program's by a relative error of at most 0.0003.
Values sent between devices are 32-bit elements; how exact they have to be, the bound alone decides.
A program may use at most 192 MiB of HBM per device.

```python
import math
import jax
import jax.numpy as jnp
from jax import lax

CX = 16
CY = 32
NZ = 512
PART_DEV = 2048
LEVELS = 4
RADIUS = 2
TERMS = 3
NX = 512
NY = 256
PARTICLES = 524288
N_GX = 32
N_GY = 8


def draw_cells(key, part):
    devices = N_GX * N_GY
    block_cells = CX * CY * NZ
    flat_cells = jax.random.randint(key, (devices, PART_DEV), 0, block_cells)
    flat_cells = flat_cells.at[:, 0].set(0)
    flat_cells = flat_cells.at[:, PART_DEV - 1].set(block_cells - 1)
    flat_cells = jnp.sort(flat_cells, axis=1)
    owner = jnp.arange(devices, dtype=jnp.int32)[:, None]
    first = owner // N_GY * CX + flat_cells // (CY * NZ)
    second = owner % N_GY * CY + flat_cells // NZ % CY
    third = flat_cells % NZ
    return jnp.stack([first.reshape(-1), second.reshape(-1), third.reshape(-1)]).astype(jnp.int32)


def levels(key, shape, pieces, low, top_value):
    factor_of, own = 1.0, jax.random.fold_in(key, 6)
    for axis_at, blocks in pieces:
        steps = jnp.exp(jax.random.uniform(jax.random.fold_in(own, axis_at), (blocks,), jnp.float32, low / len(pieces), top_value / len(pieces)))
        factor_of = factor_of * jnp.repeat(steps, shape[axis_at] // blocks).reshape([-1 if axis == axis_at else 1 for axis in range(len(shape))])
    return factor_of


def scatter_about(own_key, extent, spread, bound, pieces=(), kind=jnp.bfloat16):
    drawn = spread * jax.random.normal(own_key, extent, jnp.float32)
    if pieces:
        drawn = drawn * levels(own_key, extent, pieces, -0.22, 0.18)
    return jnp.clip(drawn, -bound, bound).astype(kind)


def setup_inputs(seed: int = 0) -> dict:
    key_list = jax.random.split(jax.random.key(seed), 6)
    cells = draw_cells(jax.random.fold_in(key_list[5], 71), 0)
    offsets = jnp.clip(1.0 * jax.random.uniform(key_list[1], (3, PARTICLES), jnp.float32) ** levels(key_list[1], (3, PARTICLES), ((1, 256),), -0.2, 0.2), 0.0, 1.0)
    charges = scatter_about(key_list[2], (PARTICLES,), 1.0, 4.0, ((0, 256),), jnp.float32)
    kernel_weights = jnp.clip(jnp.exp(jax.random.uniform(key_list[3], (LEVELS, TERMS), jnp.float32, math.log(0.25), math.log(1.0))), 0.25, 1.0)
    screening = jnp.clip(jnp.exp(jax.random.uniform(key_list[4], (1,), jnp.float32, math.log(0.1), math.log(0.4))), 0.1, 0.4)
    return dict(cells=cells, offsets=offsets, charges=charges, kernel_weights=kernel_weights, screening=screening)


widths_table = (1.0, 1.5, 2.5)
top_weight = 0.0625

def taps_for(sigma):
    return [math.exp(-(shift_by * shift_by) / (sigma * sigma)) for shift_by in range(-RADIUS, RADIUS + 1)]

def stencil(values, weights_row, level):
    total = jnp.zeros(values.shape, jnp.float32)
    for term in range(TERMS):
        tap_list = taps_for(widths_table[term])
        moved = values
        for axis in range(3):
            running = jnp.zeros(values.shape, jnp.float32)
            for shift_by in range(-RADIUS, RADIUS + 1):
                running = running + tap_list[shift_by + RADIUS] * jnp.roll(moved, -shift_by, axis)
            moved = running
        total = total + 0.5 ** level * weights_row[term] * moved
    return total

def every_other(values, axis):
    return lax.slice_in_dim(values, 0, values.shape[axis], 2, axis)

def restrict(values):
    for axis in range(3):
        values = 0.5 * jnp.roll(values, 1, axis) + values + 0.5 * jnp.roll(values, -1, axis)
        values = every_other(values, axis)
    return values

def prolong(values):
    for axis in range(3):
        upper = 0.5 * (values + jnp.roll(values, -1, axis))
        new_shape = list(values.shape)
        new_shape[axis] = new_shape[axis] * 2
        values = jnp.stack([values, upper], axis=axis + 1).reshape(new_shape)
    return values

def wrapped_squares(count):
    steps = jnp.arange(count, dtype=jnp.int32)
    offset = (steps[:, None] - steps[None, :] + count // 2) % count - count // 2
    return (offset * offset).astype(jnp.float32)

def top_field(values, screen):
    size_x, size_y, size_z = values.shape
    dist_x = wrapped_squares(size_x)
    dist_y = wrapped_squares(size_y)
    dist_z = wrapped_squares(size_z)

    def plane(target_x):
        row_x = dist_x[target_x]
        squared = row_x[None, None, :, None, None] + dist_y[:, None, None, :, None] + dist_z[None, :, None, None, :]
        kernel = jnp.exp(-screen * jnp.sqrt(squared)) / jnp.sqrt(1.0 + squared)
        return jnp.einsum('abxyz,xyz->ab', kernel, values, precision=lax.Precision.HIGHEST)
    return top_weight * lax.map(plane, jnp.arange(size_x, dtype=jnp.int32))

def reference(cells, offsets, charges, kernel_weights, screening):
    grid_sizes = (NX, NY, NZ)
    corners = [(side_x, side_y, side_z) for side_x in (0, 1) for side_y in (0, 1) for side_z in (0, 1)]

    def flat_index(corner):
        coords = [(cells[axis] + corner[axis]) % grid_sizes[axis] for axis in range(3)]
        return ((coords[0] * NY + coords[1]) * NZ + coords[2]).astype(jnp.int32)

    def weight(axis, side):
        if side == 1:
            return offsets[axis]
        return 1.0 - offsets[axis]

    def slope(side):
        if side == 1:
            return 1.0
        return -1.0
    positions = jnp.concatenate([flat_index(corner) for corner in corners])
    amounts = jnp.concatenate([charges * weight(0, corner[0]) * weight(1, corner[1]) * weight(2, corner[2]) for corner in corners])
    values = jnp.zeros((NX * NY * NZ,), jnp.float32).at[positions].add(amounts).reshape(NX, NY, NZ)
    near_list = []
    for level in range(LEVELS):
        near_list.append(stencil(values, kernel_weights[level], level))
        values = restrict(values)
    field = top_field(values, screening[0])
    for level in reversed(range(LEVELS)):
        field = near_list[level] + prolong(field)
    flat_field = field.reshape(-1)
    potential = jnp.zeros(charges.shape, jnp.float32)
    force_list = [jnp.zeros(charges.shape, jnp.float32) for axis in range(3)]
    for corner in corners:
        sample = flat_field[flat_index(corner)]
        potential = potential + weight(0, corner[0]) * weight(1, corner[1]) * weight(2, corner[2]) * sample
        force_list[0] = force_list[0] + slope(corner[0]) * weight(1, corner[1]) * weight(2, corner[2]) * sample
        force_list[1] = force_list[1] + weight(0, corner[0]) * slope(corner[1]) * weight(2, corner[2]) * sample
        force_list[2] = force_list[2] + weight(0, corner[0]) * weight(1, corner[1]) * slope(corner[2]) * sample
    forces = jnp.stack([-charges * force_list[axis] for axis in range(3)])
    return (potential, forces)
```

```python
import math

import jax
import jax.numpy as jnp
import numpy as np
from jax import lax
from jax.experimental import pallas as pl
from jax.experimental.pallas import tpu as pltpu
from jax.sharding import PartitionSpec as P

CX, CY, NZ = 16, 32, 512
PART = 2048
CHUNK = 256
TERMS = 3
WIDTHS = (1.0, 1.5, 2.5)
TOP_WEIGHT = 0.0625
N_GX, N_GY = 32, 8
MESH = pl.DeviceIdType.MESH
F32, BF16 = jnp.float32, jnp.bfloat16

COUNT_X = (16, 8, 4, 2)
COUNT_Y = (32, 16, 8, 4)
GROUPS = (4, 2, 1, 1)
PITCH = (40, 24, 16, 16)
LANE_STEP = (1, 1, 1, 2)
NEAR_ONE = [math.exp(-1.0 / (s * s)) for s in WIDTHS]
NEAR_TWO = [math.exp(-4.0 / (s * s)) for s in WIDTHS]

FAR3 = [(dx, dy) for dx in (-2, -1, 0, 1, 2) for dy in (-1, 0, 1) if (dx, dy) != (0, 0)]

Y_OFFSET, C_OFFSET = {}, {}
for _l in range(3):
    for _t in range(3):
        for _g in range(GROUPS[_l]):
            Y_OFFSET[_l, _t, _g] = sum(
                3 * GROUPS[k] * (COUNT_X[k] + 1) for k in range(_l)
            ) + (_t * GROUPS[_l] + _g) * (COUNT_X[_l] + 1)
            C_OFFSET[_l, _t, _g] = 3 * len(C_OFFSET)
Y_ROWS = 280
C_ROWS = 64


def split(values):
    high = values.astype(BF16)
    return high, (values - high.astype(F32)).astype(BF16)


def dot3(left, right_high, right_low):
    high, low = split(left)
    return (
        jnp.dot(high, right_high, preferred_element_type=F32)
        + jnp.dot(low, right_high, preferred_element_type=F32)
        + jnp.dot(high, right_low, preferred_element_type=F32)
    )


def turn(values, shift):
    return pltpu.roll(values, shift % 128, 1)


def column_of(depth):
    return (depth & 3) * 128 + (depth >> 2)


def deposit_kernel(cells_s, cells_v, offsets_v, charges_v, out_ref):
    out_ref[...] = jnp.zeros_like(out_ref)
    pitch = PITCH[0]
    row = lax.broadcasted_iota(jnp.int32, (pitch, CHUNK), 0)
    depth_row = lax.broadcasted_iota(jnp.int32, (NZ, CHUNK), 0)
    for chunk in range(PART // CHUNK):
        part = pl.ds(chunk * CHUNK, CHUNK)
        x = cells_v[0:1, part] & (CX - 1)
        y = (cells_v[1:2, part] & (CY - 1)) + 2
        z = cells_v[2:3, part]
        fx, fy, fz = offsets_v[0:1, part], offsets_v[1:2, part], offsets_v[2:3, part]
        charge = charges_v[0:1, part]
        hot = jnp.where(depth_row == column_of(z), 1.0, 0.0).astype(BF16)
        across = jnp.where(row == y, 1.0 - fy, 0.0) + jnp.where(row == y + 1, fy, 0.0)
        first = cells_s[0, chunk * CHUNK] & (CX - 1)
        last = cells_s[0, chunk * CHUNK + CHUNK - 1] & (CX - 1)

        def plane(px, carry):
            here = jnp.where(x == px, charge, 0.0)
            low, high = here * (1.0 - fx), here * fx
            table = jnp.concatenate(
                [
                    across * (low * (1.0 - fz)),
                    across * (high * (1.0 - fz)),
                    across * (low * fz),
                    across * (high * fz),
                ],
                axis=0,
            )
            table_high, table_low = split(table)
            dims = (((1,), (1,)), ((), ()))
            spread = lax.dot_general(
                table_high, hot, dims, preferred_element_type=F32
            ) + lax.dot_general(table_low, hot, dims, preferred_element_type=F32)
            rows = pl.ds(pl.multiple_of(px * pitch, 8), 2 * pitch)
            for group in range(4):
                value = spread[: 2 * pitch, group * 128 : group * 128 + 128]
                if group:
                    above = spread[2 * pitch :, group * 128 - 128 : group * 128]
                else:
                    above = turn(spread[2 * pitch :, 384:512], 1)
                out_ref[group, rows, :] += value + above
            return carry

        lax.fori_loop(first, last + 1, plane, 0)


def sample_kernel(cells_s, cells_v, offsets_v, charges_v, field, potential, forces):
    pitch = PITCH[0]
    row = lax.broadcasted_iota(jnp.int32, (pitch, CHUNK), 0)
    depth_row = lax.broadcasted_iota(jnp.int32, (NZ, CHUNK), 0)
    for chunk in range(PART // CHUNK):
        part = pl.ds(chunk * CHUNK, CHUNK)
        x = cells_v[0:1, part] & (CX - 1)
        y = cells_v[1:2, part] & (CY - 1)
        z = cells_v[2:3, part]
        fx, fy, fz = offsets_v[0:1, part], offsets_v[1:2, part], offsets_v[2:3, part]
        hot_low = jnp.where(depth_row == column_of(z), 1.0, 0.0).astype(BF16)
        hot_high = jnp.where(depth_row == column_of((z + 1) & (NZ - 1)), 1.0, 0.0).astype(BF16)
        across = jnp.where(row == y, 1.0 - fy, 0.0) + jnp.where(row == y + 1, fy, 0.0)
        across_slope = jnp.where(row == y + 1, 1.0, 0.0) - jnp.where(row == y, 1.0, 0.0)
        first = cells_s[0, chunk * CHUNK] & (CX - 1)
        last = cells_s[0, chunk * CHUNK + CHUNK - 1] & (CX - 1)

        def plane(px, carry):
            rows = pl.ds(pl.multiple_of(px * pitch, 8), 2 * pitch)
            values = jnp.concatenate([field[group, rows, :] for group in range(4)], axis=1)
            high, low = split(values)
            at_low = jnp.dot(high, hot_low, preferred_element_type=F32) + jnp.dot(
                low, hot_low, preferred_element_type=F32
            )
            at_high = jnp.dot(high, hot_high, preferred_element_type=F32) + jnp.dot(
                low, hot_high, preferred_element_type=F32
            )
            value = (1.0 - fz) * at_low + fz * at_high
            change = at_high - at_low
            low_x, high_x = value[:pitch], value[pitch:]
            value_x = (1.0 - fx) * low_x + fx * high_x
            change_x = (1.0 - fx) * change[:pitch] + fx * change[pitch:]
            found = (
                jnp.sum(across * value_x, axis=0, keepdims=True),
                jnp.sum(across * (high_x - low_x), axis=0, keepdims=True),
                jnp.sum(across_slope * value_x, axis=0, keepdims=True),
                jnp.sum(across * change_x, axis=0, keepdims=True),
            )
            here = x == px
            return tuple(jnp.where(here, new, old) for new, old in zip(found, carry))

        nothing = jnp.zeros((1, CHUNK), F32)
        found = lax.fori_loop(first, last + 1, plane, (nothing,) * 4)
        minus = -charges_v[0:1, part]
        potential[0:1, part] = found[0]
        for axis in range(3):
            forces[axis : axis + 1, part] = minus * found[1 + axis]


def depth_sums(values, level):
    if level == 0:
        up0, up1 = turn(values[0], -1), turn(values[1], -1)
        down2, down3 = turn(values[2], 1), turn(values[3], 1)
        one = [down3 + values[1], values[0] + values[2], values[1] + values[3], values[2] + up0]
        two = [down2 + values[2], down3 + values[3], values[0] + up0, values[1] + up1]
        return one, two
    if level == 1:
        up0, up1 = turn(values[0], -1), turn(values[1], -1)
        down0, down1 = turn(values[0], 1), turn(values[1], 1)
        return [down1 + values[1], values[0] + up0], [down0 + up0, down1 + up1]
    step = LANE_STEP[level]
    value = values[0]
    return (
        [turn(value, step) + turn(value, -step)],
        [turn(value, 2 * step) + turn(value, -2 * step)],
    )


def near_depth(level, grid, mixed, first, count):
    pitch = PITCH[level]

    def plane(p, carry):
        rows = pl.ds(pl.multiple_of(p * pitch, 8), pitch)
        values = [grid[group, rows, :] for group in range(GROUPS[level])]
        one, two = depth_sums(values, level)
        for group in range(GROUPS[level]):
            for term in range(TERMS):
                mixed[term, group, rows, :] = (
                    values[group] + NEAR_ONE[term] * one[group] + NEAR_TWO[term] * two[group]
                )
        return carry

    lax.fori_loop(first, first + count, plane, 0)


def near_rest(level, mixed, weights, out, low, high):
    pitch = PITCH[level]
    blocks = -(-(COUNT_Y[level] + 1) // 8)
    scale = [0.5**level * weights[level, term] for term in range(TERMS)]
    scale_one = [scale[t] * NEAR_ONE[t] for t in range(TERMS)]
    scale_two = [scale[t] * NEAR_TWO[t] for t in range(TERMS)]

    def one_block(step, carry):
        group = step // blocks
        start = step % blocks * 8
        zero, one, two = {}, {}, {}
        for plane in range(low, high + 4):
            terms = []
            for term in range(TERMS):
                cells = [
                    mixed[term, group, pl.ds(plane * pitch + start + shift, 8), :]
                    for shift in range(5)
                ]
                terms.append(
                    cells[2]
                    + NEAR_ONE[term] * (cells[1] + cells[3])
                    + NEAR_TWO[term] * (cells[0] + cells[4])
                )
            for table, factors in ((zero, scale), (one, scale_one), (two, scale_two)):
                table[plane] = sum(factors[t] * terms[t] for t in range(1, TERMS)) + factors[0] * terms[0]
            done = plane - 4
            if done >= low:
                out[group, pl.ds(done * pitch + start, 8), :] = (
                    zero[done + 2] + (one[done + 1] + one[done + 3]) + (two[done] + two[done + 4])
                )
        return carry

    lax.fori_loop(0, GROUPS[level] * blocks, one_block, 0)


def halve(level, source, padded, store):
    pitch = PITCH[level]
    groups = GROUPS[level]
    top = COUNT_X[level]
    for plane in range(top // 2 + 1):

        def at(group, p):
            return source[group, pl.ds(p * pitch, pitch), :]

        mixed = []
        for group in range(groups):
            sides = [at(group, p) for p in (2 * plane - 1, 2 * plane + 1) if 0 <= p <= top]
            mixed.append(at(group, 2 * plane) + 0.5 * sum(sides[1:], sides[0]))
        if level == 0:
            halved = [
                mixed[0] + 0.5 * (turn(mixed[3], 1) + mixed[1]),
                mixed[2] + 0.5 * (mixed[1] + mixed[3]),
            ]
        elif level == 1:
            halved = [mixed[0] + 0.5 * (turn(mixed[1], 1) + mixed[1])]
        else:
            halved = [mixed[0] + 0.5 * (turn(mixed[0], 1) + turn(mixed[0], -1))]
        next_pitch = PITCH[level + 1]
        for group, value in enumerate(halved):
            padded[group, 8 : 8 + pitch, :] = value
            result = padded[group, pl.ds(6, next_pitch, stride=2), :] + 0.5 * (
                padded[group, pl.ds(5, next_pitch, stride=2), :]
                + padded[group, pl.ds(7, next_pitch, stride=2), :]
            )
            store(group, plane, result)


def double(level, coarse, fine):
    pitch, coarse_pitch = PITCH[level], PITCH[level + 1]
    count = pitch // 2
    last = None
    for plane in range(COUNT_X[level + 1] + 1):
        now = []
        rows = [
            [coarse[group, pl.ds(plane * coarse_pitch + shift, count), :] for shift in (0, 1)]
            for group in range(GROUPS[level + 1])
        ]
        for values in ([r[0] for r in rows], [0.5 * (r[0] + r[1]) for r in rows]):
            if level == 0:
                v0, v1 = values
                now.append([v0, 0.5 * (v0 + v1), v1, 0.5 * (v1 + turn(v0, -1))])
            elif level == 1:
                now.append([values[0], 0.5 * (values[0] + turn(values[0], -1))])
            else:
                now.append(values)
        for parity in range(2):
            for group in range(GROUPS[level]):
                if last is not None:
                    place = pl.ds((2 * plane - 1) * pitch + parity, count, stride=2)
                    fine[group, place, :] += 0.5 * (last[parity][group] + now[parity][group])
                place = pl.ds(2 * plane * pitch + parity, count, stride=2)
                fine[group, place, :] += now[parity][group]
        last = now


def field_kernel(
    weights,
    screening,
    own0,
    forward_high,
    forward_low,
    back_high,
    back_low,
    out,
    grid0,
    grid1,
    grid2,
    grid3,
    own1,
    own2,
    own3,
    field1,
    field2,
    field3,
    mixed0,
    mixed1,
    mixed2,
    mixed3,
    padded0,
    padded1,
    padded2,
    x0,
    x1,
    x2,
    y_out,
    y_in,
    c_out,
    c_in,
    in3,
    stage1,
    gathered,
    stage2,
    x_send,
    x_recv,
    y_send,
    y_recv,
    c_send,
    c_recv,
    send3,
    recv3,
    send_a,
    recv_a,
    send_b,
    recv_b,
):
    me_x, me_y = lax.axis_index("gx"), lax.axis_index("gy")

    def device(dx, dy):
        return (
            lax.rem(me_x + (dx + N_GX), N_GX) if dx else me_x,
            lax.rem(me_y + (dy + N_GY), N_GY) if dy else me_y,
        )

    peers = [(0, d) for d in range(1, N_GY)] + [(d, 0) for d in range(1, N_GX)]
    peers += [(dx, dy) for dx in (-2, -1, 1, 2) for dy in (-1, 1)]
    barrier = pltpu.get_barrier_semaphore()
    for peer in peers:
        pl.semaphore_signal(barrier, inc=1, device_id=device(*peer), device_id_type=MESH)

    own = (own0, own1, own2, own3)
    grids = (grid0, grid1, grid2, grid3)
    fields = (out, field1, field2, field3)
    mixes = (mixed0, mixed1, mixed2, mixed3)

    padded0[...] = jnp.zeros_like(padded0)
    padded1[...] = jnp.zeros_like(padded1)
    padded2[...] = jnp.zeros_like(padded2)

    def keep(level):
        def store(group, plane, value):
            pitch = PITCH[level]
            own[level][group, pl.ds(plane * pitch, pitch), :] = value
            grids[level][group, pl.ds((plane + 2) * pitch, pitch), :] = value

        return store

    halve(0, own0, padded0, keep(1))
    halve(1, own1, padded1, keep(2))
    grid3[...] = jnp.zeros_like(grid3)

    def keep3(group, plane, value):
        grid3[group, pl.ds((plane + 2) * 16, 16), :] = value
        own3[pl.ds(plane * 8, 8), :] = grid3[group, pl.ds((plane + 2) * 16 + 2, 8), :]

    halve(2, own2, padded2, keep3)
    for side in range(2):
        mixed = (
            own3[0:8, :] + 0.5 * own3[8:16, :] if side == 0 else own3[16:24, :] + 0.5 * own3[8:16, :]
        )
        mixed = mixed + 0.5 * (turn(mixed, 2) + turn(mixed, -2))
        padded2[0, 0:8, :] = jnp.zeros((8, 128), F32)
        padded2[0, 8:16, :] = mixed
        padded2[0, 16:24, :] = jnp.zeros((8, 128), F32)
        result = padded2[0, pl.ds(8, 8, stride=2), :] + 0.5 * (
            padded2[0, pl.ds(7, 8, stride=2), :] + padded2[0, pl.ds(9, 8, stride=2), :]
        )
        stage1[0, pl.ds(4 * side, 4), :] = result[0:4]

    pl.semaphore_wait(barrier, len(peers))

    sends = []

    def send(source, target, send_sem, recv_sem, dx, dy):
        copy = pltpu.make_async_remote_copy(
            src_ref=source,
            dst_ref=target,
            send_sem=send_sem,
            recv_sem=recv_sem,
            device_id=device(dx, dy),
            device_id_type=MESH,
        )
        copy.start()
        sends.append(copy)
        return copy

    copies_a = [
        send(stage1.at[0], stage1.at[d], send_a.at[d], recv_a.at[d], 0, d) for d in range(1, N_GY)
    ]
    for level in range(3):
        count = COUNT_X[level] + 1
        for term in range(3):
            for group in range(GROUPS[level]):
                for side in range(2):
                    y = term if side == 0 else COUNT_Y[level] - 2 + term
                    y_out[side, pl.ds(Y_OFFSET[level, term, group], count), :] = own[level][
                        group, pl.ds(2 + y, count, stride=PITCH[level]), :
                    ]
    copies_y = [
        send(y_out.at[side], y_in.at[1 - side], y_send.at[side], y_recv.at[side], 0, 2 * side - 1)
        for side in range(2)
    ]
    copies_3 = [
        send(own3, in3.at[k], send3.at[k], recv3.at[k], -dx, -dy) for k, (dx, dy) in enumerate(FAR3)
    ]
    for (level, term, group), place in C_OFFSET.items():
        for side_x in range(2):
            start = 0 if side_x == 0 else COUNT_X[level] - 2
            for side_y in range(2):
                c_out[2 * side_x + side_y, pl.ds(place, 3), :] = y_out[
                    side_y, pl.ds(Y_OFFSET[level, term, group] + start, 3), :
                ]
    copies_c = [
        send(
            c_out.at[k],
            c_in.at[3 - k],
            c_send.at[k],
            c_recv.at[k],
            2 * (k // 2) - 1,
            2 * (k % 2) - 1,
        )
        for k in range(4)
    ]
    copies_x = []
    for level, landing in ((2, x2), (1, x1), (0, x0)):
        pitch = PITCH[level]
        for side in range(2):
            start = 0 if side == 0 else (COUNT_X[level] - 2) * pitch
            copies_x.append(
                send(
                    own[level].at[:, pl.ds(start, 3 * pitch), :],
                    landing.at[1 - side],
                    x_send.at[2 * level + side],
                    x_recv.at[2 * level + side],
                    2 * side - 1,
                    0,
                )
            )

    line = lax.broadcasted_iota(jnp.int32, (N_GX, 512), 0)
    column = lax.broadcasted_iota(jnp.int32, (N_GX, 512), 1)
    top_y = ((column >> 5) & 3) * 4 + (column >> 7)
    top_z = column & 31
    far_x = jnp.minimum(line, N_GX - line)
    far_y = jnp.minimum(top_y, 16 - top_y)
    far_z = jnp.minimum(top_z, 32 - top_z)
    squared = (far_x * far_x + far_y * far_y + far_z * far_z).astype(F32)
    kernel = jnp.exp(-screening[0] * jnp.sqrt(squared)) / jnp.sqrt(1.0 + squared)
    kernel_hat = dot3(kernel, forward_high[...], forward_low[...])
    kernel_next = pltpu.roll(kernel_hat, N_GX - 1, 0)

    for copy in copies_a:
        copy.wait_recv()
    for side in range(2):
        for y in range(16):
            slot = (16 - y // 2 * 2) // 2 % 8
            if y % 2:
                value = stage1[slot, pl.ds(4 * side + 1, 1), :]
            else:
                value = (
                    stage1[slot, pl.ds(4 * side, 1), :]
                    + stage1[(slot + 1) % 8, pl.ds(4 * side + 2, 1), :]
                )
            gathered[y // 4, pl.ds(4 * side + y % 4, 1), :] = value
    packed = jnp.concatenate([gathered[q] for q in range(4)], axis=1)
    source = lax.broadcasted_iota(jnp.int32, (512, 128), 0)
    target = lax.broadcasted_iota(jnp.int32, (512, 128), 1)
    place = jnp.where(source == (target >> 5) * 128 + (target & 31) * 4, 1.0, 0.0).astype(BF16)
    packed_high, packed_low = split(packed)
    packed = jnp.dot(packed_high, place, preferred_element_type=F32) + jnp.dot(
        packed_low, place, preferred_element_type=F32
    )
    stage2[pl.ds(0, 8), :] = packed
    stage2[pl.ds(N_GX * 8, 8), :] = packed
    copies_b = [
        send(
            stage2.at[pl.ds(0, 8), :],
            stage2.at[pl.ds(8 * d, 8), :],
            send_b.at[d],
            recv_b.at[d],
            d,
            0,
        )
        for d in range(1, N_GX)
    ]

    grid0[:, pl.ds(2 * PITCH[0], 17 * PITCH[0]), :] = own0[...]
    for level in range(4):
        rows = mixes[level].shape[2]
        for group in range(GROUPS[level]):
            for term in range(TERMS):
                mixes[level][term, group, pl.ds(rows - 8, 8), :] = jnp.zeros((8, 128), F32)
    for copy in copies_y:
        copy.wait_recv()
    for level in range(3):
        pitch, count = PITCH[level], COUNT_X[level] + 1
        for term in range(3):
            for group in range(GROUPS[level]):
                for side in range(2):
                    y = term - 2 if side == 0 else COUNT_Y[level] + term
                    rows = pl.ds(2 * pitch + y + 2, count, stride=pitch)
                    grids[level][group, rows, :] += y_in[
                        side, pl.ds(Y_OFFSET[level, term, group], count), :
                    ]
    near_depth(0, grid0, mixed0, 3, 15)
    near_rest(0, mixed0, weights, out, 3, 14)

    for copy in copies_3:
        copy.wait_recv()
    for k, (dx, dy) in enumerate(FAR3):
        first, count = (2, 3) if dy < 0 else (0, 3) if dy > 0 else (0, 5)
        for plane in range(3):
            x = 2 * dx + plane
            if -2 <= x <= 4:
                rows = pl.ds((x + 2) * 16 + 4 * dy + first + 2, count)
                grid3[0, rows, :] += in3[k, pl.ds(plane * 8 + first, count), :]
    near_depth(3, grid3, mixed3, 0, 7)
    near_rest(3, mixed3, weights, field3, 0, 3)
    lane = lax.broadcasted_iota(jnp.int32, (8, 128), 1)
    for plane in range(3):
        value = field3[0, pl.ds(plane * 16, 8), :]
        field3[0, pl.ds(plane * 16, 8), :] = jnp.where(
            lane % 2 == 0, value, 0.5 * (turn(value, 1) + turn(value, -1))
        )
        field3[0, pl.ds(plane * 16 + 8, 8), :] = jnp.zeros((8, 128), F32)

    for copy in copies_c:
        copy.wait_recv()
    for number, (level, landing) in enumerate(((2, x2), (1, x1), (0, x0))):
        pitch, size_x, grid = PITCH[level], COUNT_X[level], grids[level]
        for copy in copies_x[2 * number : 2 * number + 2]:
            copy.wait_recv()
        grid[:, pl.ds(0, 2 * pitch), :] = landing[0, :, pl.ds(0, 2 * pitch), :]
        grid[:, pl.ds(2 * pitch, pitch), :] += landing[0, :, pl.ds(2 * pitch, pitch), :]
        start = (size_x + 2) * pitch
        grid[:, pl.ds(start, pitch), :] += landing[1, :, pl.ds(0, pitch), :]
        grid[:, pl.ds(start + pitch, 2 * pitch), :] = landing[1, :, pl.ds(pitch, 2 * pitch), :]
        for term in range(3):
            for group in range(GROUPS[level]):
                for k in range(4):
                    x = -2 if k // 2 == 0 else size_x
                    y = term - 2 if k % 2 == 0 else COUNT_Y[level] + term
                    rows = pl.ds((x + 2) * pitch + y + 2, 3, stride=pitch)
                    grid[group, rows, :] += c_in[k, pl.ds(C_OFFSET[level, term, group], 3), :]
        if level:
            near_depth(level, grid, mixes[level], 0, size_x + 5)
            near_rest(level, mixes[level], weights, fields[level], 0, size_x + 1)
        else:
            near_depth(0, grid, mixed0, 0, 3)
            near_depth(0, grid, mixed0, 18, 3)
            near_rest(0, mixed0, weights, out, 0, 3)
            near_rest(0, mixed0, weights, out, 14, 17)

    for copy in copies_b:
        copy.wait_recv()
    planes = jnp.concatenate(
        [
            stage2[pl.ds(r, N_GX, stride=8), :] + stage2[pl.ds(12 + r, N_GX, stride=8), :]
            for r in range(4)
        ],
        axis=1,
    )
    hat = dot3(planes, forward_high[...], forward_low[...])
    low = jnp.sum(kernel_hat * hat, axis=0, keepdims=True)
    high = jnp.sum(kernel_next * hat, axis=0, keepdims=True)
    pair = jnp.concatenate([low, high, jnp.zeros((6, 512), F32)], axis=0)
    top = dot3(pair, back_high[...], back_low[...])
    rows_of = [[top[side : side + 1, b * 128 : b * 128 + 128] for b in range(3)] for side in range(2)]
    for plane in range(3):
        line_of = (
            rows_of[0]
            if plane == 0
            else rows_of[1]
            if plane == 2
            else [0.5 * (rows_of[0][b] + rows_of[1][b]) for b in range(3)]
        )
        for y in range(5):
            value = line_of[y // 2] if y % 2 == 0 else 0.5 * (line_of[y // 2] + line_of[y // 2 + 1])
            field3[0, pl.ds(plane * 16 + y, 1), :] += value
    for level in (2, 1, 0):
        double(level, fields[level + 1], fields[level])
    for copy in sends:
        copy.wait_send()


def transforms():
    def cas(size):
        angle = 2.0 * np.pi * np.outer(np.arange(size), np.arange(size)) / size
        return np.cos(angle) + np.sin(angle)

    cas_y, cas_z = cas(16), cas(32)
    source = np.arange(512)
    source_y = ((source >> 5) & 3) * 4 + (source >> 7)
    source_z = source & 31
    forward = (cas_y[source_y][:, :, None] * cas_z[source_z][:, None, :]).reshape(512, 512)
    lane = np.arange(128)
    share = (lane % 4) / 4.0
    lanes = (1.0 - share) * cas_z[:, lane // 4] + share * cas_z[:, (lane // 4 + 1) % 32]
    back = (cas_y[:, None, :3, None] * lanes[None, :, None, :]).reshape(512, 384)
    back = back * (TOP_WEIGHT / 512.0)

    def pair(values):
        high = values.astype(jnp.bfloat16)
        low = (values - high.astype(np.float64)).astype(jnp.bfloat16)
        return high, low

    return pair(forward) + pair(back)


def local(cells, offsets, charges, kernel_weights, screening):
    charges_row = charges.reshape(1, PART)
    vmem = pl.BlockSpec(memory_space=pltpu.VMEM)
    smem = pl.BlockSpec(memory_space=pltpu.SMEM)
    limit = 48 * 1024 * 1024
    grid_shape = (4, 17 * PITCH[0], 128)
    deposited = pl.pallas_call(
        deposit_kernel,
        out_shape=jax.ShapeDtypeStruct(grid_shape, F32),
        in_specs=[smem, vmem, vmem, vmem],
        out_specs=vmem,
        compiler_params=pltpu.CompilerParams(vmem_limit_bytes=limit),
        name="deposit",
    )(cells, cells, offsets, charges_row)

    def rimmed(level):
        return (GROUPS[level], (COUNT_X[level] + 5) * PITCH[level] + 8, 128)

    scratch = [pltpu.VMEM(rimmed(level), F32) for level in range(4)]
    scratch += [
        pltpu.VMEM((GROUPS[level], (COUNT_X[level] + 1) * PITCH[level], 128), F32) for level in (1, 2)
    ]
    scratch += [pltpu.VMEM((24, 128), F32)]
    scratch += [
        pltpu.VMEM((GROUPS[level], (COUNT_X[level] + 1) * PITCH[level], 128), F32)
        for level in (1, 2, 3)
    ]
    scratch += [pltpu.VMEM((TERMS,) + rimmed(level), F32) for level in range(4)]
    scratch += [pltpu.VMEM((2, 56, 128), F32), pltpu.VMEM((1, 40, 128), F32), pltpu.VMEM((1, 40, 128), F32)]
    scratch += [pltpu.VMEM((2, GROUPS[level], 3 * PITCH[level], 128), F32) for level in range(3)]
    scratch += [pltpu.VMEM((2, Y_ROWS, 128), F32)] * 2
    scratch += [pltpu.VMEM((4, C_ROWS, 128), F32)] * 2
    scratch += [
        pltpu.VMEM((len(FAR3), 24, 128), F32),
        pltpu.VMEM((N_GY, 8, 128), F32),
        pltpu.VMEM((4, 8, 128), F32),
        pltpu.VMEM(((N_GX + 1) * 8, 128), F32),
    ]
    for count in (6, 2, 4, len(FAR3), N_GY, N_GX):
        scratch += [pltpu.SemaphoreType.DMA((count,))] * 2
    field = pl.pallas_call(
        field_kernel,
        out_shape=jax.ShapeDtypeStruct(grid_shape, F32),
        in_specs=[smem, smem] + [vmem] * 5,
        out_specs=vmem,
        scratch_shapes=scratch,
        compiler_params=pltpu.CompilerParams(
            vmem_limit_bytes=limit, collective_id=0, has_side_effects=True
        ),
        name="field",
    )(kernel_weights, screening, deposited, *[jnp.asarray(t) for t in transforms()])
    potential, forces = pl.pallas_call(
        sample_kernel,
        out_shape=[
            jax.ShapeDtypeStruct((1, PART), F32),
            jax.ShapeDtypeStruct((3, PART), F32),
        ],
        in_specs=[smem] + [vmem] * 4,
        out_specs=[vmem, vmem],
        compiler_params=pltpu.CompilerParams(vmem_limit_bytes=limit),
        name="sample",
    )(cells, cells, offsets, charges_row, field)
    return (potential.reshape(PART), forces)


def solution(mesh):
    return jax.shard_map(
        local,
        mesh=mesh,
        in_specs=(P(None, ("gx", "gy")), P(None, ("gx", "gy")), P(("gx", "gy")), P(), P()),
        out_specs=(P(("gx", "gy")), P(None, ("gx", "gy"))),
        check_vma=False,
    )
```

```python
import math

import jax
import jax.numpy as jnp
import numpy as np
from jax import lax
from jax.experimental import pallas as pl
from jax.experimental.pallas import tpu as pltpu
from jax.sharding import PartitionSpec as P

CX, CY, NZ = 16, 32, 512
PART = 2048
CHUNK = 256
TERMS = 3
WIDTHS = (1.0, 1.5, 2.5)
TOP_WEIGHT = 0.0625
N_GX, N_GY = 32, 8
MESH = pl.DeviceIdType.MESH
F32, BF16 = jnp.float32, jnp.bfloat16

COUNT_X = (16, 8, 4, 2)
COUNT_Y = (32, 16, 8, 4)
GROUPS = (4, 2, 1, 1)
PITCH = (40, 24, 16, 16)
LANE_STEP = (1, 1, 1, 2)
NEAR_ONE = [math.exp(-1.0 / (s * s)) for s in WIDTHS]
NEAR_TWO = [math.exp(-4.0 / (s * s)) for s in WIDTHS]

FAR3 = [(dx, dy) for dx in (-2, -1, 0, 1, 2) for dy in (-1, 0, 1) if (dx, dy) != (0, 0)]

Y_OFFSET, C_OFFSET = {}, {}
for _l in range(3):
    for _t in range(3):
        for _g in range(GROUPS[_l]):
            Y_OFFSET[_l, _t, _g] = sum(
                3 * GROUPS[k] * (COUNT_X[k] + 1) for k in range(_l)
            ) + (_t * GROUPS[_l] + _g) * (COUNT_X[_l] + 1)
            C_OFFSET[_l, _t, _g] = 3 * len(C_OFFSET)
Y_ROWS = 280
C_ROWS = 64


def split(values):
    high = values.astype(BF16)
    return high, (values - high.astype(F32)).astype(BF16)


def dot3(left, right_high, right_low):
    high, low = split(left)
    return (
        jnp.dot(high, right_high, preferred_element_type=F32)
        + jnp.dot(low, right_high, preferred_element_type=F32)
        + jnp.dot(high, right_low, preferred_element_type=F32)
    )


def turn(values, shift):
    return pltpu.roll(values, shift % 128, 1)


def column_of(depth):
    return (depth & 3) * 128 + (depth >> 2)


def load_particles(hbm, vmem, sems):
    copies = [pltpu.make_async_copy(h, v, sems.at[k]) for k, (h, v) in enumerate(zip(hbm, vmem))]
    for copy in copies:
        copy.start()
    return copies


def plane_spans(cells_v, *lead):
    spans = []
    for chunk in range(PART // CHUNK):
        part = slice(chunk * CHUNK, (chunk + 1) * CHUNK)
        x = (cells_v[(*lead, slice(0, 1), part)] & (CX - 1)).astype(F32)
        spans.append((jnp.min(x).astype(jnp.int32), jnp.max(x).astype(jnp.int32)))
    return spans


def further_windows(spans, starts_of, width, span_s, visit):
    for chunk, (first, last) in enumerate(spans):
        span_s[2 * chunk] = starts_of(first) + width
        span_s[2 * chunk + 1] = last + 1

    def one_chunk(chunk, carry):
        start, end = span_s[2 * chunk], span_s[2 * chunk + 1]

        def one_window(step, inner):
            visit(pl.multiple_of(chunk * CHUNK, CHUNK), start + step * width)
            return inner

        windows = lax.div(jnp.maximum(end - start + width, 0), width)
        return lax.fori_loop(0, windows, one_window, carry)

    lax.fori_loop(0, PART // CHUNK, one_chunk, 0)


DEPOSIT_PLANES = 5
SAMPLE_PLANES = 6


HALO_PLANES = 3
HALO_CHUNKS = 2


def spread(cells, offsets, charge, base, start, width):
    pitch = PITCH[0]
    row = lax.broadcasted_iota(jnp.int32, (pitch, CHUNK), 0)
    depth_row = lax.broadcasted_iota(jnp.int32, (NZ, CHUNK), 0)
    plane = lax.broadcasted_iota(jnp.int32, (8, CHUNK), 0) + base
    x = cells[0] & (CX - 1)
    y = (cells[1] & (CY - 1)) + 2
    fx, fy, fz = offsets
    hot = jnp.where(depth_row == column_of(cells[2]), 1.0, 0.0).astype(BF16)
    across = jnp.where(row == y, 1.0 - fy, 0.0) + jnp.where(row == y + 1, fy, 0.0)
    share = jnp.where(plane == x, charge * (1.0 - fx), jnp.where(plane == x + 1, charge * fx, 0.0))
    share = jnp.where(plane >= start, share, 0.0)
    shares = (share * (1.0 - fz), share * fz)
    table = jnp.concatenate(
        [across * shares[side][k : k + 1] for side in range(2) for k in range(width)], axis=0
    )
    high, low = split(table)
    dims = (((1,), (1,)), ((), ()))
    total = lax.dot_general(high, hot, dims, preferred_element_type=F32) + lax.dot_general(
        low, hot, dims, preferred_element_type=F32
    )
    count = width * pitch
    values = []
    for group in range(4):
        if group:
            above = total[count:, group * 128 - 128 : group * 128]
        else:
            above = turn(total[count:, 384:512], 1)
        values.append(total[:count, group * 128 : group * 128 + 128] + above)
    return values


def rows_of(ref, part, *lead):
    return [ref[(*lead, slice(k, k + 1), part)] for k in range(3)]


def deposit_kernel(cells_h, offsets_h, charges_h, out_ref, cells_v, offsets_v, charges_v, span_s, sems):
    copies = load_particles((cells_h, offsets_h, charges_h), (cells_v, offsets_v, charges_v), sems)
    out_ref[...] = jnp.zeros_like(out_ref)
    for copy in copies:
        copy.wait()
    pitch, width = PITCH[0], DEPOSIT_PLANES

    def visit(place, start):
        part = pl.ds(place, CHUNK)
        base = jnp.minimum(start, CX + 1 - width)
        values = spread(
            rows_of(cells_v, part), rows_of(offsets_v, part), charges_v[0:1, part], base, start, width
        )
        rows = pl.ds(pl.multiple_of(base * pitch, 8), width * pitch)
        for group in range(4):
            out_ref[group, rows, :] += values[group]

    spans = plane_spans(cells_v)
    for chunk, (first, _) in enumerate(spans):
        visit(chunk * CHUNK, first)
    further_windows(spans, lambda first: first, width, span_s, visit)


def depth_sums(values, level):
    if level == 0:
        up0, up1 = turn(values[0], -1), turn(values[1], -1)
        down2, down3 = turn(values[2], 1), turn(values[3], 1)
        one = [down3 + values[1], values[0] + values[2], values[1] + values[3], values[2] + up0]
        two = [down2 + values[2], down3 + values[3], values[0] + up0, values[1] + up1]
        return one, two
    if level == 1:
        up0, up1 = turn(values[0], -1), turn(values[1], -1)
        down0, down1 = turn(values[0], 1), turn(values[1], 1)
        return [down1 + values[1], values[0] + up0], [down0 + up0, down1 + up1]
    step = LANE_STEP[level]
    value = values[0]
    return (
        [turn(value, step) + turn(value, -step)],
        [turn(value, 2 * step) + turn(value, -2 * step)],
    )


def near_depth(level, grid, mixed, first, count):
    pitch = PITCH[level]

    def plane(p, carry):
        rows = pl.ds(pl.multiple_of(p * pitch, 8), pitch)
        values = [grid[group, rows, :] for group in range(GROUPS[level])]
        one, two = depth_sums(values, level)
        for group in range(GROUPS[level]):
            for term in range(TERMS):
                mixed[term, group, rows, :] = (
                    values[group] + NEAR_ONE[term] * one[group] + NEAR_TWO[term] * two[group]
                )
        return carry

    lax.fori_loop(first, first + count, plane, 0)


def near_tail(level, mixed):
    rows = mixed.shape[2]
    for group in range(GROUPS[level]):
        for term in range(TERMS):
            mixed[term, group, pl.ds(rows - 8, 8), :] = jnp.zeros((8, 128), F32)


def near_rest(level, mixed, weights, out, low, high, shift_out=0):
    pitch = PITCH[level]
    blocks = -(-(COUNT_Y[level] + 1) // 8)
    scale = [0.5**level * weights[level, term] for term in range(TERMS)]
    scale_one = [scale[t] * NEAR_ONE[t] for t in range(TERMS)]
    scale_two = [scale[t] * NEAR_TWO[t] for t in range(TERMS)]

    def one_block(step, carry):
        group = step // blocks
        start = step % blocks * 8
        zero, one, two = {}, {}, {}
        for plane in range(low, high + 4):
            terms = []
            for term in range(TERMS):
                cells = [
                    mixed[term, group, pl.ds(plane * pitch + start + shift, 8), :]
                    for shift in range(5)
                ]
                terms.append(
                    cells[2]
                    + NEAR_ONE[term] * (cells[1] + cells[3])
                    + NEAR_TWO[term] * (cells[0] + cells[4])
                )
            for table, factors in ((zero, scale), (one, scale_one), (two, scale_two)):
                table[plane] = sum(factors[t] * terms[t] for t in range(1, TERMS)) + factors[0] * terms[0]
            done = plane - 4
            if done >= low:
                out[group, pl.ds((done + shift_out) * pitch + start, 8), :] = (
                    zero[done + 2] + (one[done + 1] + one[done + 3]) + (two[done] + two[done + 4])
                )
        return carry

    lax.fori_loop(0, GROUPS[level] * blocks, one_block, 0)


def near_pair(table_high, table_low, cells_high, cells_low, start):
    rows = pl.ds(start, 6 * PITCH[0])
    high = cells_high[rows, :]
    parts = (
        jnp.dot(table_high[...], high, preferred_element_type=F32)
        + jnp.dot(table_low[...], high, preferred_element_type=F32)
        + jnp.dot(table_high[...], cells_low[rows, :], preferred_element_type=F32)
    )
    count = 2 * PITCH[0]
    zero, one, two = [
        [parts[p * count : (p + 1) * count, g * 128 : g * 128 + 128] for g in range(4)] for p in range(3)
    ]
    return [
        zero[0] + (turn(one[3], 1) + one[1]) + (turn(two[2], 1) + two[2]),
        zero[1] + (one[0] + one[2]) + (turn(two[3], 1) + two[3]),
        zero[2] + (one[1] + one[3]) + (two[0] + turn(two[0], -1)),
        zero[3] + (one[2] + turn(one[0], -1)) + (two[1] + turn(two[1], -1)),
    ]


def halve(level, source, padded, store):
    pitch = PITCH[level]
    groups = GROUPS[level]
    top = COUNT_X[level]
    for plane in range(top // 2 + 1):

        def at(group, p):
            return source[group, pl.ds(p * pitch, pitch), :]

        mixed = []
        for group in range(groups):
            sides = [at(group, p) for p in (2 * plane - 1, 2 * plane + 1) if 0 <= p <= top]
            mixed.append(at(group, 2 * plane) + 0.5 * sum(sides[1:], sides[0]))
        if level == 0:
            halved = [
                mixed[0] + 0.5 * (turn(mixed[3], 1) + mixed[1]),
                mixed[2] + 0.5 * (mixed[1] + mixed[3]),
            ]
        elif level == 1:
            halved = [mixed[0] + 0.5 * (turn(mixed[1], 1) + mixed[1])]
        else:
            halved = [mixed[0] + 0.5 * (turn(mixed[0], 1) + turn(mixed[0], -1))]
        next_pitch = PITCH[level + 1]
        for group, value in enumerate(halved):
            padded[group, 8 : 8 + pitch, :] = value
            result = padded[group, pl.ds(6, next_pitch, stride=2), :] + 0.5 * (
                padded[group, pl.ds(5, next_pitch, stride=2), :]
                + padded[group, pl.ds(7, next_pitch, stride=2), :]
            )
            store(group, plane, result)


def double(level, coarse, fine):
    pitch, coarse_pitch = PITCH[level], PITCH[level + 1]
    count = pitch // 2
    last = None
    for plane in range(COUNT_X[level + 1] + 1):
        now = []
        rows = [
            [coarse[group, pl.ds(plane * coarse_pitch + shift, count), :] for shift in (0, 1)]
            for group in range(GROUPS[level + 1])
        ]
        for values in ([r[0] for r in rows], [0.5 * (r[0] + r[1]) for r in rows]):
            if level == 0:
                v0, v1 = values
                now.append([v0, 0.5 * (v0 + v1), v1, 0.5 * (v1 + turn(v0, -1))])
            elif level == 1:
                now.append([values[0], 0.5 * (values[0] + turn(values[0], -1))])
            else:
                now.append(values)
        for parity in range(2):
            for group in range(GROUPS[level]):
                if last is not None:
                    place = pl.ds((2 * plane - 1) * pitch + parity, count, stride=2)
                    fine[group, place, :] += 0.5 * (last[parity][group] + now[parity][group])
                place = pl.ds(2 * plane * pitch + parity, count, stride=2)
                fine[group, place, :] += now[parity][group]
        last = now


def sample_kernel(
    cells_h,
    offsets_h,
    charges_h,
    near,
    coarse,
    grid,
    table_high,
    table_low,
    beside_cells,
    beside_offsets,
    beside_charges,
    potential,
    forces,
    cells_v,
    offsets_v,
    charges_v,
    field,
    edge,
    edge_high,
    edge_low,
    high_v,
    low_v,
    span_s,
    sems,
):
    copies = load_particles((cells_h, offsets_h, charges_h), (cells_v, offsets_v, charges_v), sems)
    pitch, width = PITCH[0], SAMPLE_PLANES

    for side in range(2):
        count = (8 - side) * pitch
        edge[side, :, pl.ds(0, count), :] = grid[:, pl.ds(side * 14 * pitch, count), :]
        if side:
            edge[side, :, pl.ds(count, pitch), :] = jnp.zeros((4, pitch, 128), F32)
        target = 4 * side * pitch
        base = CX - 2 if side == 0 else 0

        def visit(chunk):
            part = pl.ds(pl.multiple_of(chunk * CHUNK, CHUNK), CHUNK)
            values = spread(
                rows_of(beside_cells, part, side),
                rows_of(beside_offsets, part, side),
                beside_charges[side, 0:1, part],
                base,
                base,
                HALO_PLANES,
            )
            for group in range(4):
                edge[side, group, pl.ds(target, HALO_PLANES * pitch), :] += values[group]

        chunks = PART // CHUNK
        spans = plane_spans(beside_cells, side)
        if side == 0:
            own_chunks = range(chunks - HALO_CHUNKS, chunks)
            passed = sum((last < CX - 3).astype(jnp.int32) for _, last in spans)
            low, high = passed, chunks - HALO_CHUNKS
        else:
            own_chunks = range(HALO_CHUNKS)
            reached = sum((first < 3).astype(jnp.int32) for first, _ in spans)
            low, high = HALO_CHUNKS, reached
        for chunk in own_chunks:
            visit(chunk)

        def more(chunk, carry):
            visit(chunk)
            return carry

        lax.fori_loop(low, high, more, 0)
        for group in range(4):
            high, low = split(edge[side, group])
            edge_high[side, :, group * 128 : group * 128 + 128] = high
            edge_low[side, :, group * 128 : group * 128 + 128] = low
        for window in range(2):
            values = near_pair(
                table_high, table_low, edge_high.at[side], edge_low.at[side], window * 2 * pitch
            )
            planes = 1 if side and window else 2
            for group in range(4):
                field[group, pl.ds((14 * side + 2 * window) * pitch, planes * pitch), :] = values[group][
                    : planes * pitch
                ]
    field[:, pl.ds(4 * pitch, 10 * pitch), :] = near[:, pl.ds(4 * pitch, 10 * pitch), :]
    double(0, coarse, field)

    for group in range(5):
        values = field[group] if group < 4 else turn(field[0], -1)
        values = jnp.concatenate([values, jnp.zeros((pitch, 128), F32)], axis=0)
        high, low = split(values)
        high_v[:, group * 128 : group * 128 + 128] = high
        low_v[:, group * 128 : group * 128 + 128] = low
    for copy in copies:
        copy.wait()
    row = lax.broadcasted_iota(jnp.int32, (8, CHUNK), 0)
    depth_row = lax.broadcasted_iota(jnp.int32, (NZ, CHUNK), 0)

    def found_in(place, start):
        part = pl.ds(place, CHUNK)
        x = cells_v[0:1, part] & (CX - 1)
        y = cells_v[1:2, part] & (CY - 1)
        z = cells_v[2:3, part]
        fx, fy, fz = offsets_v[0:1, part], offsets_v[1:2, part], offsets_v[2:3, part]
        hot = jnp.where(depth_row == column_of(z), 1.0, 0.0).astype(BF16)
        base = jnp.minimum(start, CX + 2 - width)
        rows = pl.ds(pl.multiple_of(base * pitch, 16), width * pitch)
        at_low = jnp.dot(high_v[rows, 0:512], hot, preferred_element_type=F32) + jnp.dot(
            low_v[rows, 0:512], hot, preferred_element_type=F32
        )
        at_high = jnp.dot(high_v[rows, 128:640], hot, preferred_element_type=F32) + jnp.dot(
            low_v[rows, 128:640], hot, preferred_element_type=F32
        )
        sums = [jnp.zeros((8, CHUNK), F32)] * 4
        for k in range(width):
            picks = []
            for values in (at_low, at_high):
                for side in range(2):
                    pick = jnp.zeros((8, CHUNK), F32)
                    for block in range(pitch // 8):
                        start_row = k * pitch + block * 8
                        pick = jnp.where(row + block * 8 == y + side, values[start_row : start_row + 8], pick)
                    picks.append(pick)
            change0, change1 = picks[2] - picks[0], picks[3] - picks[1]
            value0, value1 = picks[0] + fz * change0, picks[1] + fz * change1
            value = (1.0 - fy) * value0 + fy * value1
            change = (1.0 - fy) * change0 + fy * change1
            plane = base + k
            on = plane >= start
            share = jnp.where((x == plane) & on, 1.0 - fx, jnp.where((x + 1 == plane) & on, fx, 0.0))
            slope = jnp.where((x == plane) & on, -1.0, jnp.where((x + 1 == plane) & on, 1.0, 0.0))
            sums = [
                sums[0] + share * value,
                sums[1] + slope * value,
                sums[2] + share * (value1 - value0),
                sums[3] + share * change,
            ]
        return [jnp.sum(total, axis=0, keepdims=True) for total in sums]

    def first_visit(place, start):
        part = pl.ds(place, CHUNK)
        found = found_in(place, start)
        minus = -charges_v[0:1, part]
        potential[0:1, part] = found[0]
        for axis in range(3):
            forces[axis : axis + 1, part] = minus * found[1 + axis]

    def visit(place, start):
        part = pl.ds(place, CHUNK)
        found = found_in(place, start)
        minus = -charges_v[0:1, part]
        potential[0:1, part] += found[0]
        for axis in range(3):
            forces[axis : axis + 1, part] += minus * found[1 + axis]

    spans = plane_spans(cells_v)
    for chunk, (first, _) in enumerate(spans):
        first_visit(chunk * CHUNK, first & -2)
    further_windows(spans, lambda first: first & -2, width, span_s, visit)


def field_kernel(
    weights,
    screening,
    own0,
    cells_h,
    offsets_h,
    charges_h,
    forward_high_h,
    forward_low_h,
    back_high_h,
    back_low_h,
    tables_h,
    out,
    field1,
    grid0,
    table_high,
    table_low,
    beside_cells,
    beside_offsets,
    beside_charges,
    forward_high,
    forward_low,
    back_high,
    back_low,
    tables,
    cells_high,
    cells_low,
    load_sems,
    grid1,
    grid2,
    grid3,
    own1,
    own2,
    own3,
    field2,
    field3,
    mixed1,
    mixed2,
    mixed3,
    padded0,
    padded1,
    padded2,
    x1,
    x2,
    y_out,
    y_in,
    c_out,
    c_in,
    in3,
    stage1,
    gathered,
    stage2,
    p_send,
    p_recv,
    x_send,
    x_recv,
    y_send,
    y_recv,
    c_send,
    c_recv,
    send3,
    recv3,
    send_a,
    recv_a,
    send_b,
    recv_b,
):
    me_x, me_y = lax.axis_index("gx"), lax.axis_index("gy")

    def device(dx, dy):
        return (
            lax.rem(me_x + (dx + N_GX), N_GX) if dx else me_x,
            lax.rem(me_y + (dy + N_GY), N_GY) if dy else me_y,
        )

    peers = [(0, d) for d in range(1, N_GY)] + [(d, 0) for d in range(1, N_GX)]
    peers += [(dx, dy) for dx in (-2, -1, 1, 2) for dy in (-1, 1)]
    barrier = pltpu.get_barrier_semaphore()
    for peer in peers:
        pl.semaphore_signal(barrier, inc=1, device_id=device(*peer), device_id_type=MESH)

    loads = [
        pltpu.make_async_copy(h, v, load_sems.at[k])
        for k, (h, v) in enumerate(
            (
                (forward_high_h, forward_high),
                (forward_low_h, forward_low),
                (back_high_h, back_high),
                (back_low_h, back_low),
                (tables_h, tables),
            )
        )
    ]
    for load in loads:
        load.start()

    own = (own0, own1, own2, own3)
    grids = (grid0, grid1, grid2, grid3)
    fields = (out, field1, field2, field3)
    mixes = (None, mixed1, mixed2, mixed3)

    padded0[...] = jnp.zeros_like(padded0)
    padded1[...] = jnp.zeros_like(padded1)
    padded2[...] = jnp.zeros_like(padded2)

    def keep(level):
        def store(group, plane, value):
            pitch = PITCH[level]
            own[level][group, pl.ds(plane * pitch, pitch), :] = value
            grids[level][group, pl.ds((plane + 2) * pitch, pitch), :] = value

        return store

    halve(0, own0, padded0, keep(1))
    halve(1, own1, padded1, keep(2))
    grid3[...] = jnp.zeros_like(grid3)

    def keep3(group, plane, value):
        grid3[group, pl.ds((plane + 2) * 16, 16), :] = value
        own3[pl.ds(plane * 8, 8), :] = grid3[group, pl.ds((plane + 2) * 16 + 2, 8), :]

    halve(2, own2, padded2, keep3)
    for side in range(2):
        mixed = (
            own3[0:8, :] + 0.5 * own3[8:16, :] if side == 0 else own3[16:24, :] + 0.5 * own3[8:16, :]
        )
        mixed = mixed + 0.5 * (turn(mixed, 2) + turn(mixed, -2))
        padded2[0, 0:8, :] = jnp.zeros((8, 128), F32)
        padded2[0, 8:16, :] = mixed
        padded2[0, 16:24, :] = jnp.zeros((8, 128), F32)
        result = padded2[0, pl.ds(8, 8, stride=2), :] + 0.5 * (
            padded2[0, pl.ds(7, 8, stride=2), :] + padded2[0, pl.ds(9, 8, stride=2), :]
        )
        stage1[0, pl.ds(4 * side, 4), :] = result[0:4]

    pl.semaphore_wait(barrier, len(peers))

    sends = []

    def far_rows(dx):
        return pl.ds(16, 8) if dx == -2 else pl.ds(0, 8) if dx == 2 else pl.ds(0, 24)

    def send(source, target, send_sem, recv_sem, dx, dy):
        copy = pltpu.make_async_remote_copy(
            src_ref=source,
            dst_ref=target,
            send_sem=send_sem,
            recv_sem=recv_sem,
            device_id=device(dx, dy),
            device_id_type=MESH,
        )
        copy.start()
        sends.append(copy)
        return copy

    copies_a = [
        send(stage1.at[0], stage1.at[d], send_a.at[d], recv_a.at[d], 0, d) for d in range(1, N_GY)
    ]
    particles = (
        (cells_h, beside_cells),
        (offsets_h, beside_offsets),
        (charges_h, beside_charges),
    )
    copies_p = [
        send(
            source,
            landing.at[1 - side],
            p_send.at[3 * side + k],
            p_recv.at[3 * side + k],
            2 * side - 1,
            0,
        )
        for k, (source, landing) in enumerate(particles)
        for side in range(2)
    ]
    for level in range(3):
        count = COUNT_X[level] + 1
        for term in range(3):
            for group in range(GROUPS[level]):
                for side in range(2):
                    y = term if side == 0 else COUNT_Y[level] - 2 + term
                    y_out[side, pl.ds(Y_OFFSET[level, term, group], count), :] = own[level][
                        group, pl.ds(2 + y, count, stride=PITCH[level]), :
                    ]
    copies_y = [
        send(y_out.at[side], y_in.at[1 - side], y_send.at[side], y_recv.at[side], 0, 2 * side - 1)
        for side in range(2)
    ]
    copies_3 = [
        send(own3.at[far_rows(dx)], in3.at[k, far_rows(dx)], send3.at[k], recv3.at[k], -dx, -dy)
        for k, (dx, dy) in enumerate(FAR3)
    ]
    for (level, term, group), place in C_OFFSET.items():
        for side_x in range(2):
            start = 0 if side_x == 0 else COUNT_X[level] - 2
            for side_y in range(2):
                c_out[2 * side_x + side_y, pl.ds(place, 3), :] = y_out[
                    side_y, pl.ds(Y_OFFSET[level, term, group] + start, 3), :
                ]
    copies_c = [
        send(
            c_out.at[k],
            c_in.at[3 - k],
            c_send.at[k],
            c_recv.at[k],
            2 * (k // 2) - 1,
            2 * (k % 2) - 1,
        )
        for k in range(4)
    ]
    copies_x = []
    for level, landing in ((2, x2), (1, x1)):
        pitch = PITCH[level]
        for side in range(2):
            start = 0 if side == 0 else (COUNT_X[level] - 2) * pitch
            copies_x.append(
                send(
                    own[level].at[:, pl.ds(start, 3 * pitch), :],
                    landing.at[1 - side],
                    x_send.at[2 * level - 2 + side],
                    x_recv.at[2 * level - 2 + side],
                    2 * side - 1,
                    0,
                )
            )

    line = lax.broadcasted_iota(jnp.int32, (N_GX, 512), 0)
    column = lax.broadcasted_iota(jnp.int32, (N_GX, 512), 1)
    top_y = ((column >> 5) & 3) * 4 + (column >> 7)
    top_z = column & 31
    far_x = jnp.minimum(line, N_GX - line)
    far_y = jnp.minimum(top_y, 16 - top_y)
    far_z = jnp.minimum(top_z, 32 - top_z)
    squared = (far_x * far_x + far_y * far_y + far_z * far_z).astype(F32)
    kernel = jnp.exp(-screening[0] * jnp.sqrt(squared)) / jnp.sqrt(1.0 + squared)
    for load in loads[:2]:
        load.wait()
    kernel_hat = dot3(kernel, forward_high[...], forward_low[...])
    loads[4].wait()
    table = weights[0, 0] * tables[0] + weights[0, 1] * tables[1] + weights[0, 2] * tables[2]
    high, low = split(table)
    table_high[...] = high
    table_low[...] = low
    kernel_next = pltpu.roll(kernel_hat, N_GX - 1, 0)

    for copy in copies_a:
        copy.wait_recv()
    for side in range(2):
        for y in range(16):
            slot = (16 - y // 2 * 2) // 2 % 8
            if y % 2:
                value = stage1[slot, pl.ds(4 * side + 1, 1), :]
            else:
                value = (
                    stage1[slot, pl.ds(4 * side, 1), :]
                    + stage1[(slot + 1) % 8, pl.ds(4 * side + 2, 1), :]
                )
            gathered[y // 4, pl.ds(4 * side + y % 4, 1), :] = value
    packed = jnp.concatenate([gathered[q] for q in range(4)], axis=1)
    source = lax.broadcasted_iota(jnp.int32, (512, 128), 0)
    target = lax.broadcasted_iota(jnp.int32, (512, 128), 1)
    place = jnp.where(source == (target >> 5) * 128 + (target & 31) * 4, 1.0, 0.0).astype(BF16)
    packed_high, packed_low = split(packed)
    packed = jnp.dot(packed_high, place, preferred_element_type=F32) + jnp.dot(
        packed_low, place, preferred_element_type=F32
    )
    stage2[pl.ds(0, 8), :] = packed
    stage2[pl.ds(N_GX * 8, 8), :] = packed
    copies_b = [
        send(
            stage2.at[pl.ds(0, 8), :],
            stage2.at[pl.ds(8 * d, 8), :],
            send_b.at[d],
            recv_b.at[d],
            d,
            0,
        )
        for d in range(1, N_GX)
    ]

    for start, count in ((0, 2), (19, 2)):
        grid0[:, pl.ds(start * PITCH[0], count * PITCH[0]), :] = jnp.zeros((4, count * PITCH[0], 128), F32)
    grid0[:, pl.ds(2 * PITCH[0], 17 * PITCH[0]), :] = own0[...]
    for level in range(1, 4):
        near_tail(level, mixes[level])
    for copy in copies_y:
        copy.wait_recv()
    for level in range(3):
        pitch, count = PITCH[level], COUNT_X[level] + 1
        for term in range(3):
            for group in range(GROUPS[level]):
                for side in range(2):
                    y = term - 2 if side == 0 else COUNT_Y[level] + term
                    rows = pl.ds(2 * pitch + y + 2, count, stride=pitch)
                    grids[level][group, rows, :] += y_in[
                        side, pl.ds(Y_OFFSET[level, term, group], count), :
                    ]
    for group in range(4):
        high, low = split(grid0[group, pl.ds(4 * PITCH[0], 14 * PITCH[0]), :])
        cells_high[:, group * 128 : group * 128 + 128] = high
        cells_low[:, group * 128 : group * 128 + 128] = low
    for window in range(5):
        values = near_pair(table_high, table_low, cells_high, cells_low, window * 2 * PITCH[0])
        for group in range(4):
            out[group, pl.ds((4 + 2 * window) * PITCH[0], 2 * PITCH[0]), :] = values[group]

    for copy in copies_3:
        copy.wait_recv()
    for k, (dx, dy) in enumerate(FAR3):
        first, count = (2, 3) if dy < 0 else (0, 3) if dy > 0 else (0, 5)
        for plane in range(3):
            x = 2 * dx + plane
            if -2 <= x <= 4:
                rows = pl.ds((x + 2) * 16 + 4 * dy + first + 2, count)
                grid3[0, rows, :] += in3[k, pl.ds(plane * 8 + first, count), :]
    near_depth(3, grid3, mixed3, 0, 7)
    near_rest(3, mixed3, weights, field3, 0, 3)
    lane = lax.broadcasted_iota(jnp.int32, (8, 128), 1)
    for plane in range(3):
        value = field3[0, pl.ds(plane * 16, 8), :]
        field3[0, pl.ds(plane * 16, 8), :] = jnp.where(
            lane % 2 == 0, value, 0.5 * (turn(value, 1) + turn(value, -1))
        )
        field3[0, pl.ds(plane * 16 + 8, 8), :] = jnp.zeros((8, 128), F32)

    for copy in copies_c:
        copy.wait_recv()

    def add_corners(level):
        for term in range(3):
            for group in range(GROUPS[level]):
                for k in range(4):
                    x = -2 if k // 2 == 0 else COUNT_X[level]
                    y = term - 2 if k % 2 == 0 else COUNT_Y[level] + term
                    rows = pl.ds((x + 2) * PITCH[level] + y + 2, 3, stride=PITCH[level])
                    grids[level][group, rows, :] += c_in[k, pl.ds(C_OFFSET[level, term, group], 3), :]

    add_corners(0)
    for number, (level, landing) in enumerate(((2, x2), (1, x1))):
        pitch, size_x, grid = PITCH[level], COUNT_X[level], grids[level]
        for copy in copies_x[2 * number : 2 * number + 2]:
            copy.wait_recv()
        grid[:, pl.ds(0, 2 * pitch), :] = landing[0, :, pl.ds(0, 2 * pitch), :]
        grid[:, pl.ds(2 * pitch, pitch), :] += landing[0, :, pl.ds(2 * pitch, pitch), :]
        start = (size_x + 2) * pitch
        grid[:, pl.ds(start, pitch), :] += landing[1, :, pl.ds(0, pitch), :]
        grid[:, pl.ds(start + pitch, 2 * pitch), :] = landing[1, :, pl.ds(pitch, 2 * pitch), :]
        add_corners(level)
        near_depth(level, grid, mixes[level], 0, size_x + 5)
        near_rest(level, mixes[level], weights, fields[level], 0, size_x + 1)

    for copy in copies_b:
        copy.wait_recv()
    planes = jnp.concatenate(
        [
            stage2[pl.ds(r, N_GX, stride=8), :] + stage2[pl.ds(12 + r, N_GX, stride=8), :]
            for r in range(4)
        ],
        axis=1,
    )
    hat = dot3(planes, forward_high[...], forward_low[...])
    low = jnp.sum(kernel_hat * hat, axis=0, keepdims=True)
    high = jnp.sum(kernel_next * hat, axis=0, keepdims=True)
    pair = jnp.concatenate([low, high, jnp.zeros((6, 512), F32)], axis=0)
    for load in loads[2:4]:
        load.wait()
    top = dot3(pair, back_high[...], back_low[...])
    ends = [[top[side : side + 1, b * 128 : b * 128 + 128] for b in range(3)] for side in range(2)]
    for plane in range(3):
        line_of = (
            ends[0]
            if plane == 0
            else ends[1]
            if plane == 2
            else [0.5 * (ends[0][b] + ends[1][b]) for b in range(3)]
        )
        for y in range(5):
            value = line_of[y // 2] if y % 2 == 0 else 0.5 * (line_of[y // 2] + line_of[y // 2 + 1])
            field3[0, pl.ds(plane * 16 + y, 1), :] += value
    for level in (2, 1):
        double(level, fields[level + 1], fields[level])
    for copy in copies_p:
        copy.wait_recv()
    for copy in sends:
        copy.wait_send()


def transforms():
    def cas(size):
        angle = 2.0 * np.pi * np.outer(np.arange(size), np.arange(size)) / size
        return np.cos(angle) + np.sin(angle)

    cas_y, cas_z = cas(16), cas(32)
    source = np.arange(512)
    source_y = ((source >> 5) & 3) * 4 + (source >> 7)
    source_z = source & 31
    forward = (cas_y[source_y][:, :, None] * cas_z[source_z][:, None, :]).reshape(512, 512)
    lane = np.arange(128)
    share = (lane % 4) / 4.0
    lanes = (1.0 - share) * cas_z[:, lane // 4] + share * cas_z[:, (lane // 4 + 1) % 32]
    back = (cas_y[:, None, :3, None] * lanes[None, :, None, :]).reshape(512, 384)
    back = back * (TOP_WEIGHT / 512.0)

    def pair(values):
        high = values.astype(jnp.bfloat16)
        low = (values - high.astype(np.float64)).astype(jnp.bfloat16)
        return high, low

    return pair(forward) + pair(back)


def near_tables():
    pitch = PITCH[0]
    tables = np.zeros((TERMS, 3, 2, pitch, 6, pitch))
    for term, width in enumerate(WIDTHS):
        for apart in range(3):
            for a in range(-2, 3):
                for b in range(-2, 3):
                    value = math.exp(-(apart * apart + a * a + b * b) / (width * width))
                    for plane in range(2):
                        for y in range(COUNT_Y[0] + 1):
                            tables[term, apart, plane, y, plane + 2 + a, y + 2 + b] = value
    return tables.reshape(TERMS, 6 * pitch, 6 * pitch).astype(np.float32)


def local(cells, offsets, charges, kernel_weights, screening):
    def in_hbm(*arrays):
        return [pltpu.with_memory_space_constraint(array, pltpu.HBM) for array in arrays]

    held = in_hbm(cells, offsets, charges.reshape(1, PART))
    vmem = pl.BlockSpec(memory_space=pltpu.VMEM)
    smem = pl.BlockSpec(memory_space=pltpu.SMEM)
    hbm = pl.BlockSpec(memory_space=pltpu.HBM)
    limit = 48 * 1024 * 1024
    grid_shape = (4, 17 * PITCH[0], 128)
    particles = [
        pltpu.VMEM((3, PART), jnp.int32),
        pltpu.VMEM((3, PART), F32),
        pltpu.VMEM((1, PART), F32),
    ]
    spans = [pltpu.SMEM((2 * PART // CHUNK,), jnp.int32), pltpu.SemaphoreType.DMA((3,))]
    deposited = pl.pallas_call(
        deposit_kernel,
        out_shape=jax.ShapeDtypeStruct(grid_shape, F32),
        in_specs=[hbm, hbm, hbm],
        out_specs=vmem,
        scratch_shapes=particles + spans,
        compiler_params=pltpu.CompilerParams(vmem_limit_bytes=limit),
        name="deposit",
    )(*held)

    def rimmed(level):
        return (GROUPS[level], (COUNT_X[level] + 5) * PITCH[level] + 8, 128)

    scratch = [pltpu.VMEM((512, 512), BF16)] * 2 + [pltpu.VMEM((512, 384), BF16)] * 2
    scratch += [pltpu.VMEM((TERMS, 6 * PITCH[0], 6 * PITCH[0]), F32)]
    scratch += [pltpu.VMEM((14 * PITCH[0], 512), BF16)] * 2
    scratch += [pltpu.SemaphoreType.DMA((5,))]
    scratch += [pltpu.VMEM(rimmed(level), F32) for level in (1, 2, 3)]
    scratch += [
        pltpu.VMEM((GROUPS[level], (COUNT_X[level] + 1) * PITCH[level], 128), F32) for level in (1, 2)
    ]
    scratch += [pltpu.VMEM((24, 128), F32)]
    scratch += [
        pltpu.VMEM((GROUPS[level], (COUNT_X[level] + 1) * PITCH[level], 128), F32)
        for level in (2, 3)
    ]
    scratch += [pltpu.VMEM((TERMS,) + rimmed(level), F32) for level in (1, 2, 3)]
    scratch += [pltpu.VMEM((2, 56, 128), F32), pltpu.VMEM((1, 40, 128), F32), pltpu.VMEM((1, 40, 128), F32)]
    scratch += [pltpu.VMEM((2, GROUPS[level], 3 * PITCH[level], 128), F32) for level in (1, 2)]
    scratch += [pltpu.VMEM((2, Y_ROWS, 128), F32)] * 2
    scratch += [pltpu.VMEM((4, C_ROWS, 128), F32)] * 2
    scratch += [
        pltpu.VMEM((len(FAR3), 24, 128), F32),
        pltpu.VMEM((N_GY, 8, 128), F32),
        pltpu.VMEM((4, 8, 128), F32),
        pltpu.VMEM(((N_GX + 1) * 8, 128), F32),
    ]
    for count in (6, 4, 2, 4, len(FAR3), N_GY, N_GX):
        scratch += [pltpu.SemaphoreType.DMA((count,))] * 2
    given = pl.pallas_call(
        field_kernel,
        out_shape=[
            jax.ShapeDtypeStruct(grid_shape, F32),
            jax.ShapeDtypeStruct((GROUPS[1], (COUNT_X[1] + 1) * PITCH[1], 128), F32),
            jax.ShapeDtypeStruct(rimmed(0), F32),
            jax.ShapeDtypeStruct((6 * PITCH[0], 6 * PITCH[0]), BF16),
            jax.ShapeDtypeStruct((6 * PITCH[0], 6 * PITCH[0]), BF16),
            jax.ShapeDtypeStruct((2, 3, PART), jnp.int32),
            jax.ShapeDtypeStruct((2, 3, PART), F32),
            jax.ShapeDtypeStruct((2, 1, PART), F32),
        ],
        in_specs=[smem, smem, vmem] + [hbm] * 8,
        out_specs=[vmem] * 8,
        scratch_shapes=scratch,
        compiler_params=pltpu.CompilerParams(
            vmem_limit_bytes=limit, collective_id=0, has_side_effects=True
        ),
        name="field",
    )(kernel_weights, screening, deposited, *held, *in_hbm(*[jnp.asarray(t) for t in (*transforms(), near_tables())]))
    potential, forces = pl.pallas_call(
        sample_kernel,
        out_shape=[
            jax.ShapeDtypeStruct((1, PART), F32),
            jax.ShapeDtypeStruct((3, PART), F32),
        ],
        in_specs=[hbm, hbm, hbm] + [vmem] * 8,
        out_specs=[vmem, vmem],
        scratch_shapes=particles
        + [
            pltpu.VMEM(grid_shape, F32),
            pltpu.VMEM((2, 4, 8 * PITCH[0], 128), F32),
            pltpu.VMEM((2, 8 * PITCH[0], 512), BF16),
            pltpu.VMEM((2, 8 * PITCH[0], 512), BF16),
        ]
        + [pltpu.VMEM((18 * PITCH[0], 640), BF16)] * 2 + spans,
        compiler_params=pltpu.CompilerParams(vmem_limit_bytes=limit),
        name="sample",
    )(*held, *given)
    return (potential.reshape(PART), forces)


def solution(mesh):
    return jax.shard_map(
        local,
        mesh=mesh,
        in_specs=(P(None, ("gx", "gy")), P(None, ("gx", "gy")), P(("gx", "gy")), P(), P()),
        out_specs=(P(("gx", "gy")), P(None, ("gx", "gy"))),
        check_vma=False,
    )
```

```python
import math

import jax
import jax.numpy as jnp
import numpy as np
from jax import lax
from jax.experimental import pallas as pl
from jax.experimental.pallas import tpu as pltpu
from jax.sharding import PartitionSpec as P

CX, CY, NZ = 16, 32, 512
PART = 2048
CHUNK = 256
TERMS = 3
WIDTHS = (1.0, 1.5, 2.5)
TOP_WEIGHT = 0.0625
N_GX, N_GY = 32, 8
MESH = pl.DeviceIdType.MESH
F32, BF16 = jnp.float32, jnp.bfloat16

COUNT_X = (16, 8, 4, 2)
COUNT_Y = (32, 16, 8, 4)
GROUPS = (4, 2, 1, 1)
PITCH = (40, 24, 16, 16)
LANE_STEP = (1, 1, 1, 2)
NEAR_ONE = [math.exp(-1.0 / (s * s)) for s in WIDTHS]
NEAR_TWO = [math.exp(-4.0 / (s * s)) for s in WIDTHS]

FAR3 = [(dx, dy) for dx in (-2, -1, 0, 1, 2) for dy in (-1, 0, 1) if (dx, dy) != (0, 0)]

Y_OFFSET, C_OFFSET = {}, {}
for _l in range(3):
    for _t in range(3):
        for _g in range(GROUPS[_l]):
            Y_OFFSET[_l, _t, _g] = sum(
                3 * GROUPS[k] * (COUNT_X[k] + 1) for k in range(_l)
            ) + (_t * GROUPS[_l] + _g) * (COUNT_X[_l] + 1)
            C_OFFSET[_l, _t, _g] = 3 * len(C_OFFSET)
Y_ROWS = 280
C_ROWS = 64


def split(values):
    high = values.astype(BF16)
    return high, (values - high.astype(F32)).astype(BF16)


def dot3(left, right_high, right_low):
    high, low = split(left)
    return (
        jnp.dot(high, right_high, preferred_element_type=F32)
        + jnp.dot(low, right_high, preferred_element_type=F32)
        + jnp.dot(high, right_low, preferred_element_type=F32)
    )


def turn(values, shift):
    return pltpu.roll(values, shift % 128, 1)


def column_of(depth):
    return (depth & 3) * 128 + (depth >> 2)


def load_particles(hbm, vmem, sems):
    copies = [pltpu.make_async_copy(h, v, sems.at[k]) for k, (h, v) in enumerate(zip(hbm, vmem))]
    for copy in copies:
        copy.start()
    return copies


def plane_spans(cells_v, *lead):
    spans = []
    for chunk in range(PART // CHUNK):
        part = slice(chunk * CHUNK, (chunk + 1) * CHUNK)
        x = (cells_v[(*lead, slice(0, 1), part)] & (CX - 1)).astype(F32)
        spans.append((jnp.min(x).astype(jnp.int32), jnp.max(x).astype(jnp.int32)))
    return spans


def further_windows(spans, starts_of, width, span_s, visit):
    for chunk, (first, last) in enumerate(spans):
        span_s[2 * chunk] = starts_of(first) + width
        span_s[2 * chunk + 1] = last + 1

    def one_chunk(chunk, carry):
        start, end = span_s[2 * chunk], span_s[2 * chunk + 1]

        def one_window(step, inner):
            visit(pl.multiple_of(chunk * CHUNK, CHUNK), start + step * width)
            return inner

        windows = lax.div(jnp.maximum(end - start + width, 0), width)
        return lax.fori_loop(0, windows, one_window, carry)

    lax.fori_loop(0, PART // CHUNK, one_chunk, 0)


DEPOSIT_PLANES = 5
SAMPLE_PLANES = 6


HALO_PLANES = 3
HALO_CHUNKS = 2


def spread(cells, offsets, charge, base, start, width):
    pitch = PITCH[0]
    row = lax.broadcasted_iota(jnp.int32, (pitch, CHUNK), 0)
    depth_row = lax.broadcasted_iota(jnp.int32, (NZ, CHUNK), 0)
    plane = lax.broadcasted_iota(jnp.int32, (8, CHUNK), 0) + base
    x = cells[0] & (CX - 1)
    y = (cells[1] & (CY - 1)) + 2
    fx, fy, fz = offsets
    hot = jnp.where(depth_row == column_of(cells[2]), 1.0, 0.0).astype(BF16)
    across = jnp.where(row == y, 1.0 - fy, 0.0) + jnp.where(row == y + 1, fy, 0.0)
    share = jnp.where(plane == x, charge * (1.0 - fx), jnp.where(plane == x + 1, charge * fx, 0.0))
    share = jnp.where(plane >= start, share, 0.0)
    shares = (share * (1.0 - fz), share * fz)
    table = jnp.concatenate(
        [across * shares[side][k : k + 1] for side in range(2) for k in range(width)], axis=0
    )
    high, low = split(table)
    dims = (((1,), (1,)), ((), ()))
    total = lax.dot_general(high, hot, dims, preferred_element_type=F32) + lax.dot_general(
        low, hot, dims, preferred_element_type=F32
    )
    count = width * pitch
    values = []
    for group in range(4):
        if group:
            above = total[count:, group * 128 - 128 : group * 128]
        else:
            above = turn(total[count:, 384:512], 1)
        values.append(total[:count, group * 128 : group * 128 + 128] + above)
    return values


def rows_of(ref, part, *lead):
    return [ref[(*lead, slice(k, k + 1), part)] for k in range(3)]


def deposit_kernel(cells_h, offsets_h, charges_h, out_ref, cells_v, offsets_v, charges_v, span_s, sems):
    copies = load_particles((cells_h, offsets_h, charges_h), (cells_v, offsets_v, charges_v), sems)
    out_ref[...] = jnp.zeros_like(out_ref)
    for copy in copies:
        copy.wait()
    pitch, width = PITCH[0], DEPOSIT_PLANES

    def visit(place, start):
        part = pl.ds(place, CHUNK)
        base = jnp.minimum(start, CX + 1 - width)
        values = spread(
            rows_of(cells_v, part), rows_of(offsets_v, part), charges_v[0:1, part], base, start, width
        )
        rows = pl.ds(pl.multiple_of(base * pitch, 8), width * pitch)
        for group in range(4):
            out_ref[group, rows, :] += values[group]

    spans = plane_spans(cells_v)
    for chunk, (first, _) in enumerate(spans):
        visit(chunk * CHUNK, first)
    further_windows(spans, lambda first: first, width, span_s, visit)


def depth_sums(values, level):
    if level == 0:
        up0, up1 = turn(values[0], -1), turn(values[1], -1)
        down2, down3 = turn(values[2], 1), turn(values[3], 1)
        one = [down3 + values[1], values[0] + values[2], values[1] + values[3], values[2] + up0]
        two = [down2 + values[2], down3 + values[3], values[0] + up0, values[1] + up1]
        return one, two
    if level == 1:
        up0, up1 = turn(values[0], -1), turn(values[1], -1)
        down0, down1 = turn(values[0], 1), turn(values[1], 1)
        return [down1 + values[1], values[0] + up0], [down0 + up0, down1 + up1]
    step = LANE_STEP[level]
    value = values[0]
    return (
        [turn(value, step) + turn(value, -step)],
        [turn(value, 2 * step) + turn(value, -2 * step)],
    )


def near_depth(level, grid, mixed, first, count):
    pitch = PITCH[level]

    def plane(p, carry):
        rows = pl.ds(pl.multiple_of(p * pitch, 8), pitch)
        values = [grid[group, rows, :] for group in range(GROUPS[level])]
        one, two = depth_sums(values, level)
        for group in range(GROUPS[level]):
            for term in range(TERMS):
                mixed[term, group, rows, :] = (
                    values[group] + NEAR_ONE[term] * one[group] + NEAR_TWO[term] * two[group]
                )
        return carry

    lax.fori_loop(first, first + count, plane, 0)


def near_tail(level, mixed):
    rows = mixed.shape[2]
    for group in range(GROUPS[level]):
        for term in range(TERMS):
            mixed[term, group, pl.ds(rows - 8, 8), :] = jnp.zeros((8, 128), F32)


def near_rest(level, mixed, weights, out, low, high, shift_out=0):
    pitch = PITCH[level]
    blocks = -(-(COUNT_Y[level] + 1) // 8)
    scale = [0.5**level * weights[level, term] for term in range(TERMS)]
    scale_one = [scale[t] * NEAR_ONE[t] for t in range(TERMS)]
    scale_two = [scale[t] * NEAR_TWO[t] for t in range(TERMS)]

    def one_block(step, carry):
        group = step // blocks
        start = step % blocks * 8
        zero, one, two = {}, {}, {}
        for plane in range(low, high + 4):
            terms = []
            for term in range(TERMS):
                cells = [
                    mixed[term, group, pl.ds(plane * pitch + start + shift, 8), :]
                    for shift in range(5)
                ]
                terms.append(
                    cells[2]
                    + NEAR_ONE[term] * (cells[1] + cells[3])
                    + NEAR_TWO[term] * (cells[0] + cells[4])
                )
            for table, factors in ((zero, scale), (one, scale_one), (two, scale_two)):
                table[plane] = sum(factors[t] * terms[t] for t in range(1, TERMS)) + factors[0] * terms[0]
            done = plane - 4
            if done >= low:
                out[group, pl.ds((done + shift_out) * pitch + start, 8), :] = (
                    zero[done + 2] + (one[done + 1] + one[done + 3]) + (two[done] + two[done + 4])
                )
        return carry

    lax.fori_loop(0, GROUPS[level] * blocks, one_block, 0)


def near_pair(table_high, table_low, cells_high, cells_low, start):
    rows = pl.ds(start, 6 * PITCH[0])
    high = cells_high[rows, :]
    parts = (
        jnp.dot(table_high[...], high, preferred_element_type=F32)
        + jnp.dot(table_low[...], high, preferred_element_type=F32)
        + jnp.dot(table_high[...], cells_low[rows, :], preferred_element_type=F32)
    )
    count = 2 * PITCH[0]
    zero, one, two = [
        [parts[p * count : (p + 1) * count, g * 128 : g * 128 + 128] for g in range(4)] for p in range(3)
    ]
    return [
        zero[0] + (turn(one[3], 1) + one[1]) + (turn(two[2], 1) + two[2]),
        zero[1] + (one[0] + one[2]) + (turn(two[3], 1) + two[3]),
        zero[2] + (one[1] + one[3]) + (two[0] + turn(two[0], -1)),
        zero[3] + (one[2] + turn(one[0], -1)) + (two[1] + turn(two[1], -1)),
    ]


def halve(level, source, padded, store):
    pitch = PITCH[level]
    groups = GROUPS[level]
    top = COUNT_X[level]
    for plane in range(top // 2 + 1):

        def at(group, p):
            return source[group, pl.ds(p * pitch, pitch), :]

        mixed = []
        for group in range(groups):
            sides = [at(group, p) for p in (2 * plane - 1, 2 * plane + 1) if 0 <= p <= top]
            mixed.append(at(group, 2 * plane) + 0.5 * sum(sides[1:], sides[0]))
        if level == 0:
            halved = [
                mixed[0] + 0.5 * (turn(mixed[3], 1) + mixed[1]),
                mixed[2] + 0.5 * (mixed[1] + mixed[3]),
            ]
        elif level == 1:
            halved = [mixed[0] + 0.5 * (turn(mixed[1], 1) + mixed[1])]
        else:
            halved = [mixed[0] + 0.5 * (turn(mixed[0], 1) + turn(mixed[0], -1))]
        next_pitch = PITCH[level + 1]
        for group, value in enumerate(halved):
            padded[group, 8 : 8 + pitch, :] = value
            result = padded[group, pl.ds(6, next_pitch, stride=2), :] + 0.5 * (
                padded[group, pl.ds(5, next_pitch, stride=2), :]
                + padded[group, pl.ds(7, next_pitch, stride=2), :]
            )
            store(group, plane, result)


def double(level, coarse, fine):
    pitch, coarse_pitch = PITCH[level], PITCH[level + 1]
    count = pitch // 2
    last = None
    for plane in range(COUNT_X[level + 1] + 1):
        now = []
        rows = [
            [coarse[group, pl.ds(plane * coarse_pitch + shift, count), :] for shift in (0, 1)]
            for group in range(GROUPS[level + 1])
        ]
        for values in ([r[0] for r in rows], [0.5 * (r[0] + r[1]) for r in rows]):
            if level == 0:
                v0, v1 = values
                now.append([v0, 0.5 * (v0 + v1), v1, 0.5 * (v1 + turn(v0, -1))])
            elif level == 1:
                now.append([values[0], 0.5 * (values[0] + turn(values[0], -1))])
            else:
                now.append(values)
        for parity in range(2):
            for group in range(GROUPS[level]):
                if last is not None:
                    place = pl.ds((2 * plane - 1) * pitch + parity, count, stride=2)
                    fine[group, place, :] += 0.5 * (last[parity][group] + now[parity][group])
                place = pl.ds(2 * plane * pitch + parity, count, stride=2)
                fine[group, place, :] += now[parity][group]
        last = now


def halo_chunk(edge, beside_cells, beside_offsets, beside_charges, side, chunk):
    part = pl.ds(pl.multiple_of(chunk * CHUNK, CHUNK), CHUNK)
    base = CX - 2 if side == 0 else 0
    values = spread(
        rows_of(beside_cells, part, side),
        rows_of(beside_offsets, part, side),
        beside_charges[side, 0:1, part],
        base,
        base,
        HALO_PLANES,
    )
    for group in range(4):
        edge[side, group, pl.ds(4 * side * PITCH[0], HALO_PLANES * PITCH[0]), :] += values[group]


def near_edge(side, edge, edge_high, edge_low, table_high, table_low, store):
    pitch = PITCH[0]
    for group in range(4):
        high, low = split(edge[side, group])
        edge_high[side, :, group * 128 : group * 128 + 128] = high
        edge_low[side, :, group * 128 : group * 128 + 128] = low
    for window in range(2):
        values = near_pair(table_high, table_low, edge_high.at[side], edge_low.at[side], window * 2 * pitch)
        planes = 1 if side and window else 2
        store(
            pl.ds((14 * side + 2 * window) * pitch, planes * pitch),
            [value[: planes * pitch] for value in values],
        )


def sample_kernel(
    cells_h,
    offsets_h,
    charges_h,
    near,
    coarse,
    table_high,
    table_low,
    beside_cells,
    beside_offsets,
    beside_charges,
    potential,
    forces,
    cells_v,
    offsets_v,
    charges_v,
    field,
    edge,
    edge_high,
    edge_low,
    high_v,
    low_v,
    span_s,
    sems,
):
    copies = load_particles((cells_h, offsets_h, charges_h), (cells_v, offsets_v, charges_v), sems)
    pitch, width = PITCH[0], SAMPLE_PLANES

    field[...] = near[...]
    double(0, coarse, field)

    chunks = PART // CHUNK

    def planes_of(side, chunk):
        part = slice(chunk * CHUNK, (chunk + 1) * CHUNK)
        return (beside_cells[side, 0:1, part] & (CX - 1)).astype(F32)

    more_low = jnp.max(planes_of(0, chunks - HALO_CHUNKS - 1)) >= CX - HALO_PLANES
    more_high = jnp.min(planes_of(1, HALO_CHUNKS)) < HALO_PLANES

    @pl.when(more_low | more_high)
    def _():
        for side in range(2):
            edge[side] = jnp.zeros_like(edge[side])
            first = 0 if side == 0 else HALO_CHUNKS

            def one_chunk(chunk, carry):
                halo_chunk(edge, beside_cells, beside_offsets, beside_charges, side, chunk)
                return carry

            lax.fori_loop(first, first + chunks - HALO_CHUNKS, one_chunk, 0)

            def store(rows, values):
                for group in range(4):
                    field[group, rows, :] += values[group]

            near_edge(side, edge, edge_high, edge_low, table_high, table_low, store)

    for group in range(5):
        values = field[group] if group < 4 else turn(field[0], -1)
        values = jnp.concatenate([values, jnp.zeros((pitch, 128), F32)], axis=0)
        high, low = split(values)
        high_v[:, group * 128 : group * 128 + 128] = high
        low_v[:, group * 128 : group * 128 + 128] = low
    for copy in copies:
        copy.wait()
    row = lax.broadcasted_iota(jnp.int32, (8, CHUNK), 0)
    depth_row = lax.broadcasted_iota(jnp.int32, (NZ, CHUNK), 0)

    def found_in(place, start):
        part = pl.ds(place, CHUNK)
        x = cells_v[0:1, part] & (CX - 1)
        y = cells_v[1:2, part] & (CY - 1)
        z = cells_v[2:3, part]
        fx, fy, fz = offsets_v[0:1, part], offsets_v[1:2, part], offsets_v[2:3, part]
        hot = jnp.where(depth_row == column_of(z), 1.0, 0.0).astype(BF16)
        base = jnp.minimum(start, CX + 2 - width)
        rows = pl.ds(pl.multiple_of(base * pitch, 16), width * pitch)
        at_low = jnp.dot(high_v[rows, 0:512], hot, preferred_element_type=F32) + jnp.dot(
            low_v[rows, 0:512], hot, preferred_element_type=F32
        )
        at_high = jnp.dot(high_v[rows, 128:640], hot, preferred_element_type=F32) + jnp.dot(
            low_v[rows, 128:640], hot, preferred_element_type=F32
        )
        sums = [jnp.zeros((8, CHUNK), F32)] * 4
        for k in range(width):
            picks = []
            for values in (at_low, at_high):
                for side in range(2):
                    pick = jnp.zeros((8, CHUNK), F32)
                    for block in range(pitch // 8):
                        start_row = k * pitch + block * 8
                        pick = jnp.where(row + block * 8 == y + side, values[start_row : start_row + 8], pick)
                    picks.append(pick)
            change0, change1 = picks[2] - picks[0], picks[3] - picks[1]
            value0, value1 = picks[0] + fz * change0, picks[1] + fz * change1
            value = (1.0 - fy) * value0 + fy * value1
            change = (1.0 - fy) * change0 + fy * change1
            plane = base + k
            on = plane >= start
            share = jnp.where((x == plane) & on, 1.0 - fx, jnp.where((x + 1 == plane) & on, fx, 0.0))
            slope = jnp.where((x == plane) & on, -1.0, jnp.where((x + 1 == plane) & on, 1.0, 0.0))
            sums = [
                sums[0] + share * value,
                sums[1] + slope * value,
                sums[2] + share * (value1 - value0),
                sums[3] + share * change,
            ]
        return [jnp.sum(total, axis=0, keepdims=True) for total in sums]

    def first_visit(place, start):
        part = pl.ds(place, CHUNK)
        found = found_in(place, start)
        minus = -charges_v[0:1, part]
        potential[0:1, part] = found[0]
        for axis in range(3):
            forces[axis : axis + 1, part] = minus * found[1 + axis]

    def visit(place, start):
        part = pl.ds(place, CHUNK)
        found = found_in(place, start)
        minus = -charges_v[0:1, part]
        potential[0:1, part] += found[0]
        for axis in range(3):
            forces[axis : axis + 1, part] += minus * found[1 + axis]

    spans = plane_spans(cells_v)
    for chunk, (first, _) in enumerate(spans):
        first_visit(chunk * CHUNK, first & -2)
    further_windows(spans, lambda first: first & -2, width, span_s, visit)


def field_kernel(
    weights,
    screening,
    own0,
    cells_h,
    offsets_h,
    charges_h,
    forward_high_h,
    forward_low_h,
    back_high_h,
    back_low_h,
    tables_h,
    out,
    field1,
    table_high,
    table_low,
    beside_cells,
    beside_offsets,
    beside_charges,
    grid0,
    edge,
    edge_high,
    edge_low,
    forward_high,
    forward_low,
    back_high,
    back_low,
    tables,
    cells_high,
    cells_low,
    load_sems,
    grid1,
    grid2,
    grid3,
    own1,
    own2,
    own3,
    field2,
    field3,
    mixed1,
    mixed2,
    mixed3,
    padded0,
    padded1,
    padded2,
    x1,
    x2,
    y_out,
    y_in,
    c_out,
    c_in,
    in3,
    stage1,
    gathered,
    stage2,
    p_send,
    p_recv,
    x_send,
    x_recv,
    y_send,
    y_recv,
    c_send,
    c_recv,
    send3,
    recv3,
    send_a,
    recv_a,
    send_b,
    recv_b,
):
    me_x, me_y = lax.axis_index("gx"), lax.axis_index("gy")

    def device(dx, dy):
        return (
            lax.rem(me_x + (dx + N_GX), N_GX) if dx else me_x,
            lax.rem(me_y + (dy + N_GY), N_GY) if dy else me_y,
        )

    peers = [(0, d) for d in range(1, N_GY)] + [(d, 0) for d in range(1, N_GX)]
    peers += [(dx, dy) for dx in (-2, -1, 1, 2) for dy in (-1, 1)]
    barrier = pltpu.get_barrier_semaphore()
    for peer in peers:
        pl.semaphore_signal(barrier, inc=1, device_id=device(*peer), device_id_type=MESH)

    loads = [
        pltpu.make_async_copy(h, v, load_sems.at[k])
        for k, (h, v) in enumerate(
            (
                (forward_high_h, forward_high),
                (forward_low_h, forward_low),
                (back_high_h, back_high),
                (back_low_h, back_low),
                (tables_h, tables),
            )
        )
    ]
    for load in loads:
        load.start()

    own = (own0, own1, own2, own3)
    grids = (grid0, grid1, grid2, grid3)
    fields = (out, field1, field2, field3)
    mixes = (None, mixed1, mixed2, mixed3)

    padded0[...] = jnp.zeros_like(padded0)
    padded1[...] = jnp.zeros_like(padded1)
    padded2[...] = jnp.zeros_like(padded2)

    def keep(level):
        def store(group, plane, value):
            pitch = PITCH[level]
            own[level][group, pl.ds(plane * pitch, pitch), :] = value
            grids[level][group, pl.ds((plane + 2) * pitch, pitch), :] = value

        return store

    halve(0, own0, padded0, keep(1))
    halve(1, own1, padded1, keep(2))
    grid3[...] = jnp.zeros_like(grid3)

    def keep3(group, plane, value):
        grid3[group, pl.ds((plane + 2) * 16, 16), :] = value
        own3[pl.ds(plane * 8, 8), :] = grid3[group, pl.ds((plane + 2) * 16 + 2, 8), :]

    halve(2, own2, padded2, keep3)
    for side in range(2):
        mixed = (
            own3[0:8, :] + 0.5 * own3[8:16, :] if side == 0 else own3[16:24, :] + 0.5 * own3[8:16, :]
        )
        mixed = mixed + 0.5 * (turn(mixed, 2) + turn(mixed, -2))
        padded2[0, 0:8, :] = jnp.zeros((8, 128), F32)
        padded2[0, 8:16, :] = mixed
        padded2[0, 16:24, :] = jnp.zeros((8, 128), F32)
        result = padded2[0, pl.ds(8, 8, stride=2), :] + 0.5 * (
            padded2[0, pl.ds(7, 8, stride=2), :] + padded2[0, pl.ds(9, 8, stride=2), :]
        )
        stage1[0, pl.ds(4 * side, 4), :] = result[0:4]

    for level in range(3):
        count = COUNT_X[level] + 1
        for term in range(3):
            for group in range(GROUPS[level]):
                for side in range(2):
                    y = term if side == 0 else COUNT_Y[level] - 2 + term
                    y_out[side, pl.ds(Y_OFFSET[level, term, group], count), :] = own[level][
                        group, pl.ds(2 + y, count, stride=PITCH[level]), :
                    ]
    for (level, term, group), place in C_OFFSET.items():
        for side_x in range(2):
            start = 0 if side_x == 0 else COUNT_X[level] - 2
            for side_y in range(2):
                c_out[2 * side_x + side_y, pl.ds(place, 3), :] = y_out[
                    side_y, pl.ds(Y_OFFSET[level, term, group] + start, 3), :
                ]
    line = lax.broadcasted_iota(jnp.int32, (N_GX, 512), 0)
    column = lax.broadcasted_iota(jnp.int32, (N_GX, 512), 1)
    top_y = ((column >> 5) & 3) * 4 + (column >> 7)
    top_z = column & 31
    far_x = jnp.minimum(line, N_GX - line)
    far_y = jnp.minimum(top_y, 16 - top_y)
    far_z = jnp.minimum(top_z, 32 - top_z)
    squared = (far_x * far_x + far_y * far_y + far_z * far_z).astype(F32)
    kernel = jnp.exp(-screening[0, 0] * jnp.sqrt(squared)) / jnp.sqrt(1.0 + squared)
    for load in loads[:2]:
        load.wait()
    kernel_hat = dot3(kernel, forward_high[...], forward_low[...])
    loads[4].wait()
    table = weights[0, 0] * tables[0] + weights[0, 1] * tables[1] + weights[0, 2] * tables[2]
    high, low = split(table)
    table_high[...] = high
    table_low[...] = low
    kernel_next = pltpu.roll(kernel_hat, N_GX - 1, 0)
    for start, count in ((0, 2), (19, 2)):
        grid0[:, pl.ds(start * PITCH[0], count * PITCH[0]), :] = jnp.zeros((4, count * PITCH[0], 128), F32)
    grid0[:, pl.ds(2 * PITCH[0], 17 * PITCH[0]), :] = own0[...]
    for level in range(1, 4):
        near_tail(level, mixes[level])
    edge[...] = jnp.zeros_like(edge)

    pl.semaphore_wait(barrier, len(peers))

    sends = []

    def far_rows(dx):
        return pl.ds(16, 8) if dx == -2 else pl.ds(0, 8) if dx == 2 else pl.ds(0, 24)

    def send(source, target, send_sem, recv_sem, dx, dy):
        copy = pltpu.make_async_remote_copy(
            src_ref=source,
            dst_ref=target,
            send_sem=send_sem,
            recv_sem=recv_sem,
            device_id=device(dx, dy),
            device_id_type=MESH,
        )
        copy.start()
        sends.append(copy)
        return copy

    copies_a = [
        send(stage1.at[0], stage1.at[d], send_a.at[d], recv_a.at[d], 0, d) for d in range(1, N_GY)
    ]
    particles = (
        (cells_h, beside_cells),
        (offsets_h, beside_offsets),
        (charges_h, beside_charges),
    )
    copies_p = [
        send(
            source,
            landing.at[1 - side],
            p_send.at[3 * side + k],
            p_recv.at[3 * side + k],
            2 * side - 1,
            0,
        )
        for k, (source, landing) in enumerate(particles)
        for side in range(2)
    ]
    copies_c = [
        send(
            c_out.at[k],
            c_in.at[3 - k],
            c_send.at[k],
            c_recv.at[k],
            2 * (k // 2) - 1,
            2 * (k % 2) - 1,
        )
        for k in range(4)
    ]
    copies_y = [
        send(y_out.at[side], y_in.at[1 - side], y_send.at[side], y_recv.at[side], 0, 2 * side - 1)
        for side in range(2)
    ]
    copies_x = []
    for level, landing in ((1, x1), (2, x2)):
        pitch = PITCH[level]
        for side in range(2):
            start = 0 if side == 0 else (COUNT_X[level] - 2) * pitch
            copies_x.append(
                send(
                    own[level].at[:, pl.ds(start, 3 * pitch), :],
                    landing.at[1 - side],
                    x_send.at[2 * level - 2 + side],
                    x_recv.at[2 * level - 2 + side],
                    2 * side - 1,
                    0,
                )
            )

    copies_3 = [
        send(own3.at[far_rows(dx)], in3.at[k, far_rows(dx)], send3.at[k], recv3.at[k], -dx, -dy)
        for k, (dx, dy) in enumerate(FAR3)
    ]
    for copy in copies_a:
        copy.wait_recv()
    for side in range(2):
        for y in range(16):
            slot = (16 - y // 2 * 2) // 2 % 8
            if y % 2:
                value = stage1[slot, pl.ds(4 * side + 1, 1), :]
            else:
                value = (
                    stage1[slot, pl.ds(4 * side, 1), :]
                    + stage1[(slot + 1) % 8, pl.ds(4 * side + 2, 1), :]
                )
            gathered[y // 4, pl.ds(4 * side + y % 4, 1), :] = value
    packed = jnp.concatenate([gathered[q] for q in range(4)], axis=1)
    source = lax.broadcasted_iota(jnp.int32, (512, 128), 0)
    target = lax.broadcasted_iota(jnp.int32, (512, 128), 1)
    place = jnp.where(source == (target >> 5) * 128 + (target & 31) * 4, 1.0, 0.0).astype(BF16)
    packed_high, packed_low = split(packed)
    packed = jnp.dot(packed_high, place, preferred_element_type=F32) + jnp.dot(
        packed_low, place, preferred_element_type=F32
    )
    stage2[pl.ds(0, 8), :] = packed
    stage2[pl.ds(N_GX * 8, 8), :] = packed
    copies_b = [
        send(
            stage2.at[pl.ds(0, 8), :],
            stage2.at[pl.ds(8 * d, 8), :],
            send_b.at[d],
            recv_b.at[d],
            d,
            0,
        )
        for d in range(1, N_GX)
    ]

    for copy in copies_y:
        copy.wait_recv()
    for level in range(3):
        pitch, count = PITCH[level], COUNT_X[level] + 1
        for term in range(3):
            for group in range(GROUPS[level]):
                for side in range(2):
                    y = term - 2 if side == 0 else COUNT_Y[level] + term
                    rows = pl.ds(2 * pitch + y + 2, count, stride=pitch)
                    grids[level][group, rows, :] += y_in[
                        side, pl.ds(Y_OFFSET[level, term, group], count), :
                    ]
    for group in range(4):
        high, low = split(grid0[group, pl.ds(4 * PITCH[0], 14 * PITCH[0]), :])
        cells_high[:, group * 128 : group * 128 + 128] = high
        cells_low[:, group * 128 : group * 128 + 128] = low
    for window in range(5):
        values = near_pair(table_high, table_low, cells_high, cells_low, window * 2 * PITCH[0])
        for group in range(4):
            out[group, pl.ds((4 + 2 * window) * PITCH[0], 2 * PITCH[0]), :] = values[group]

    for copy in copies_p:
        copy.wait_recv()
    chunks = PART // CHUNK
    for side in range(2):
        for k in range(HALO_CHUNKS):
            chunk = chunks - 1 - k if side == 0 else k
            halo_chunk(edge, beside_cells, beside_offsets, beside_charges, side, chunk)

    for copy in copies_c:
        copy.wait_recv()

    def add_corners(level):
        for term in range(3):
            for group in range(GROUPS[level]):
                for k in range(4):
                    x = -2 if k // 2 == 0 else COUNT_X[level]
                    y = term - 2 if k % 2 == 0 else COUNT_Y[level] + term
                    rows = pl.ds((x + 2) * PITCH[level] + y + 2, 3, stride=PITCH[level])
                    grids[level][group, rows, :] += c_in[k, pl.ds(C_OFFSET[level, term, group], 3), :]

    add_corners(0)
    pitch = PITCH[0]
    for side in range(2):
        count = (8 - side) * pitch
        edge[side, :, pl.ds(0, count), :] += grid0[:, pl.ds(side * 14 * pitch, count), :]

        def store(rows, values):
            for group in range(4):
                out[group, rows, :] = values[group]

        near_edge(side, edge, edge_high, edge_low, table_high, table_low, store)
    for number, (level, landing) in enumerate(((1, x1), (2, x2))):
        pitch, size_x, grid = PITCH[level], COUNT_X[level], grids[level]
        for copy in copies_x[2 * number : 2 * number + 2]:
            copy.wait_recv()
        grid[:, pl.ds(0, 2 * pitch), :] = landing[0, :, pl.ds(0, 2 * pitch), :]
        grid[:, pl.ds(2 * pitch, pitch), :] += landing[0, :, pl.ds(2 * pitch, pitch), :]
        start = (size_x + 2) * pitch
        grid[:, pl.ds(start, pitch), :] += landing[1, :, pl.ds(0, pitch), :]
        grid[:, pl.ds(start + pitch, 2 * pitch), :] = landing[1, :, pl.ds(pitch, 2 * pitch), :]
        add_corners(level)
        near_depth(level, grid, mixes[level], 0, size_x + 5)
        near_rest(level, mixes[level], weights, fields[level], 0, size_x + 1)

    for copy in copies_3:
        copy.wait_recv()
    for k, (dx, dy) in enumerate(FAR3):
        first, count = (2, 3) if dy < 0 else (0, 3) if dy > 0 else (0, 5)
        for plane in range(3):
            x = 2 * dx + plane
            if -2 <= x <= 4:
                rows = pl.ds((x + 2) * 16 + 4 * dy + first + 2, count)
                grid3[0, rows, :] += in3[k, pl.ds(plane * 8 + first, count), :]
    near_depth(3, grid3, mixed3, 0, 7)
    near_rest(3, mixed3, weights, field3, 0, 3)
    lane = lax.broadcasted_iota(jnp.int32, (8, 128), 1)
    for plane in range(3):
        value = field3[0, pl.ds(plane * 16, 8), :]
        field3[0, pl.ds(plane * 16, 8), :] = jnp.where(
            lane % 2 == 0, value, 0.5 * (turn(value, 1) + turn(value, -1))
        )
        field3[0, pl.ds(plane * 16 + 8, 8), :] = jnp.zeros((8, 128), F32)

    for level in (2, 1):
        double(level, fields[level + 1], fields[level])

    for copy in copies_b:
        copy.wait_recv()
    planes = jnp.concatenate(
        [
            stage2[pl.ds(r, N_GX, stride=8), :] + stage2[pl.ds(12 + r, N_GX, stride=8), :]
            for r in range(4)
        ],
        axis=1,
    )
    hat = dot3(planes, forward_high[...], forward_low[...])
    low = jnp.sum(kernel_hat * hat, axis=0, keepdims=True)
    high = jnp.sum(kernel_next * hat, axis=0, keepdims=True)
    pair = jnp.concatenate([low, high, jnp.zeros((6, 512), F32)], axis=0)
    for load in loads[2:4]:
        load.wait()
    top = dot3(pair, back_high[...], back_low[...])
    row = lax.broadcasted_iota(jnp.int32, (PITCH[1], 128), 0)
    hats = [jnp.maximum(8 - jnp.abs(row - 8 * b), 0).astype(F32) * 0.125 for b in range(3)]
    for group in range(2):
        levels = [top[:, b * 128 : b * 128 + 128] for b in range(3)]
        if group:
            levels = [0.5 * (v + turn(v, -1)) for v in levels]
        low, high = [
            hats[0] * levels[0][side : side + 1]
            + hats[1] * levels[1][side : side + 1]
            + hats[2] * levels[2][side : side + 1]
            for side in range(2)
        ]
        step = 0.125 * (high - low)
        for plane in range(COUNT_X[1] + 1):
            field1[group, pl.ds(plane * PITCH[1], PITCH[1]), :] += low + float(plane) * step
    for copy in sends:
        copy.wait_send()


def transforms():
    def cas(size):
        angle = 2.0 * np.pi * np.outer(np.arange(size), np.arange(size)) / size
        return np.cos(angle) + np.sin(angle)

    cas_y, cas_z = cas(16), cas(32)
    source = np.arange(512)
    source_y = ((source >> 5) & 3) * 4 + (source >> 7)
    source_z = source & 31
    forward = (cas_y[source_y][:, :, None] * cas_z[source_z][:, None, :]).reshape(512, 512)
    lane = np.arange(128)
    share = (lane % 4) / 4.0
    lanes = (1.0 - share) * cas_z[:, lane // 4] + share * cas_z[:, (lane // 4 + 1) % 32]
    back = (cas_y[:, None, :3, None] * lanes[None, :, None, :]).reshape(512, 384)
    back = back * (TOP_WEIGHT / 512.0)

    def pair(values):
        high = values.astype(jnp.bfloat16)
        low = (values - high.astype(np.float64)).astype(jnp.bfloat16)
        return high, low

    return pair(forward) + pair(back)


def near_tables():
    pitch = PITCH[0]
    tables = np.zeros((TERMS, 3, 2, pitch, 6, pitch))
    for term, width in enumerate(WIDTHS):
        for apart in range(3):
            for a in range(-2, 3):
                for b in range(-2, 3):
                    value = math.exp(-(apart * apart + a * a + b * b) / (width * width))
                    for plane in range(2):
                        for y in range(COUNT_Y[0] + 1):
                            tables[term, apart, plane, y, plane + 2 + a, y + 2 + b] = value
    return tables.reshape(TERMS, 6 * pitch, 6 * pitch).astype(np.float32)


def local(cells, offsets, charges, kernel_weights, screening):
    def in_hbm(*arrays):
        return [pltpu.with_memory_space_constraint(array, pltpu.HBM) for array in arrays]

    held = in_hbm(cells, offsets, charges.reshape(1, PART))
    vmem = pl.BlockSpec(memory_space=pltpu.VMEM)
    smem = pl.BlockSpec(memory_space=pltpu.SMEM)
    hbm = pl.BlockSpec(memory_space=pltpu.HBM)
    limit = 48 * 1024 * 1024
    grid_shape = (4, 17 * PITCH[0], 128)
    particles = [
        pltpu.VMEM((3, PART), jnp.int32),
        pltpu.VMEM((3, PART), F32),
        pltpu.VMEM((1, PART), F32),
    ]
    spans = [pltpu.SMEM((2 * PART // CHUNK,), jnp.int32), pltpu.SemaphoreType.DMA((3,))]
    deposited = pl.pallas_call(
        deposit_kernel,
        out_shape=jax.ShapeDtypeStruct(grid_shape, F32),
        in_specs=[hbm, hbm, hbm],
        out_specs=vmem,
        scratch_shapes=particles + spans,
        compiler_params=pltpu.CompilerParams(vmem_limit_bytes=limit),
        name="deposit",
    )(*held)

    def rimmed(level):
        return (GROUPS[level], (COUNT_X[level] + 5) * PITCH[level] + 8, 128)

    scratch = [pltpu.VMEM(rimmed(0), F32)]
    edges = [pltpu.VMEM((2, 4, 8 * PITCH[0], 128), F32)]
    edges += [pltpu.VMEM((2, 8 * PITCH[0], 512), BF16)] * 2
    scratch += edges
    scratch += [pltpu.VMEM((512, 512), BF16)] * 2 + [pltpu.VMEM((512, 384), BF16)] * 2
    scratch += [pltpu.VMEM((TERMS, 6 * PITCH[0], 6 * PITCH[0]), F32)]
    scratch += [pltpu.VMEM((14 * PITCH[0], 512), BF16)] * 2
    scratch += [pltpu.SemaphoreType.DMA((5,))]
    scratch += [pltpu.VMEM(rimmed(level), F32) for level in (1, 2, 3)]
    scratch += [
        pltpu.VMEM((GROUPS[level], (COUNT_X[level] + 1) * PITCH[level], 128), F32) for level in (1, 2)
    ]
    scratch += [pltpu.VMEM((24, 128), F32)]
    scratch += [
        pltpu.VMEM((GROUPS[level], (COUNT_X[level] + 1) * PITCH[level], 128), F32)
        for level in (2, 3)
    ]
    scratch += [pltpu.VMEM((TERMS,) + rimmed(level), F32) for level in (1, 2, 3)]
    scratch += [pltpu.VMEM((2, 56, 128), F32), pltpu.VMEM((1, 40, 128), F32), pltpu.VMEM((1, 40, 128), F32)]
    scratch += [pltpu.VMEM((2, GROUPS[level], 3 * PITCH[level], 128), F32) for level in (1, 2)]
    scratch += [pltpu.VMEM((2, Y_ROWS, 128), F32)] * 2
    scratch += [pltpu.VMEM((4, C_ROWS, 128), F32)] * 2
    scratch += [
        pltpu.VMEM((len(FAR3), 24, 128), F32),
        pltpu.VMEM((N_GY, 8, 128), F32),
        pltpu.VMEM((4, 8, 128), F32),
        pltpu.VMEM(((N_GX + 1) * 8, 128), F32),
    ]
    for count in (6, 4, 2, 4, len(FAR3), N_GY, N_GX):
        scratch += [pltpu.SemaphoreType.DMA((count,))] * 2
    given = pl.pallas_call(
        field_kernel,
        out_shape=[
            jax.ShapeDtypeStruct(grid_shape, F32),
            jax.ShapeDtypeStruct((GROUPS[1], (COUNT_X[1] + 1) * PITCH[1], 128), F32),
            jax.ShapeDtypeStruct((6 * PITCH[0], 6 * PITCH[0]), BF16),
            jax.ShapeDtypeStruct((6 * PITCH[0], 6 * PITCH[0]), BF16),
            jax.ShapeDtypeStruct((2, 3, PART), jnp.int32),
            jax.ShapeDtypeStruct((2, 3, PART), F32),
            jax.ShapeDtypeStruct((2, 1, PART), F32),
        ],
        in_specs=[smem, smem, vmem] + [hbm] * 8,
        out_specs=[vmem] * 7,
        scratch_shapes=scratch,
        compiler_params=pltpu.CompilerParams(
            vmem_limit_bytes=limit, collective_id=0, has_side_effects=True
        ),
        name="field",
    )(kernel_weights, screening.reshape(1, 1), deposited, *held, *in_hbm(*[jnp.asarray(t) for t in (*transforms(), near_tables())]))
    potential, forces = pl.pallas_call(
        sample_kernel,
        out_shape=[
            jax.ShapeDtypeStruct((1, PART), F32),
            jax.ShapeDtypeStruct((3, PART), F32),
        ],
        in_specs=[hbm, hbm, hbm] + [vmem] * 7,
        out_specs=[vmem, vmem],
        scratch_shapes=particles
        + [pltpu.VMEM(grid_shape, F32)]
        + edges
        + [pltpu.VMEM((18 * PITCH[0], 640), BF16)] * 2 + spans,
        compiler_params=pltpu.CompilerParams(vmem_limit_bytes=limit),
        name="sample",
    )(*held, *given)
    return (potential.reshape(PART), forces)


def solution(mesh):
    return jax.shard_map(
        local,
        mesh=mesh,
        in_specs=(P(None, ("gx", "gy")), P(None, ("gx", "gy")), P(("gx", "gy")), P(), P()),
        out_specs=(P(("gx", "gy")), P(None, ("gx", "gy"))),
        check_vma=False,
    )
```
